512 devices in a mesh: grad: 16 (over z, core), flow: 8 (over y_hi, x), vort: 4 (over y_lo).
Axes of the slice: x: 4, y: 8 (y_hi: 2, y_lo: 4; y = y_hi * 4 + y_lo), z: 8, core: 2. Of those that a mesh axis runs over, the one named last changes fastest.
Arguments:
- populations: float32 [19, 128, 128, 512], P(None, 'grad', 'flow', 'vort'), as said below
- thermal_noise: bfloat16 [15, 128, 128, 512], P(None, 'grad', 'flow', 'vort'), may hold values from -4 to 4
- relax_rates: float32 [15], replicated, may hold values from 0.4 to 1.8
- plane_shift: int32 [16], replicated, may hold values from 0 to 127
- fraction_index: int32 [1], replicated, may hold values from 1 to 7
- plane_speed: float32 [16], replicated, may hold values from 0.05 to 0.15
Outputs:
- read: float32 [19, 128, 128, 512], P(None, 'grad', 'flow', 'vort')
The draws below stay inside these ranges and needn't reach their ends.
Inputs may be any that keep to these rules, and one draw needn't show every extreme that they name: `populations`: every value lies between 0.4 and 1.8. plane_shift[g] belongs to the plane between gradient slab g - 1 and slab g; plane 0 joins the last slab and the first.
All inputs are finite; a program needn't handle non-finite values.
Results may differ from the reference program's by a relative error of at most 0.0003.
Values sent between devices are 32-bit elements; how exact they have to be, the bound alone decides.
A program may use at most 64 MiB of HBM per device.

```python
import math
import jax
import jax.numpy as jnp
import numpy as np
from jax import lax

Q = 19
MODES = 15
FRACS = 8
CY = 8
NY = 128
NX = 128
NZ = 512
N_GRAD = 16


def draw_populations(key, part):
    key = jax.random.fold_in(key, 11)
    values = jax.random.normal(key, (Q, NY, NX, NZ), jnp.float32)
    return 1.0 + 0.2 * jnp.clip(values, -2.5, 2.5)


def set_ends(values, rng, least, high):
    spot = [jax.random.randint(jax.random.fold_in(rng, axis), (), 0, length) for axis, length in enumerate(values.shape)]
    widest = values.shape.index(max(values.shape))
    beside = spot[:widest] + [(spot[widest] + 1) % values.shape[widest]] + spot[widest + 1:]
    return values.at[tuple(spot)].set(least).at[tuple(beside)].set(high)


def shard_levels(rng, shape, shards, least, largest):
    factor_of, own = 1.0, jax.random.fold_in(rng, 6)
    for dim, blocks in shards:
        heights = jnp.exp(jax.random.uniform(jax.random.fold_in(own, dim), (blocks,), jnp.float32, least / len(shards), largest / len(shards)))
        factor_of = factor_of * jnp.repeat(heights, shape[dim] // blocks).reshape([-1 if axis == dim else 1 for axis in range(len(shape))])
    return factor_of


def bell_draw(stream_key, dims, deviation, bound, cuts=(), kind=jnp.bfloat16):
    entries = deviation * jax.random.normal(stream_key, dims, jnp.float32)
    if cuts:
        entries = entries * shard_levels(stream_key, dims, cuts, -0.22, 0.18)
    return jnp.clip(entries, -bound, bound).astype(kind)


def setup_inputs(seed: int = 0) -> dict:
    seeds = jax.random.split(jax.random.key(seed), 7)
    return {
        "populations": draw_populations(jax.random.fold_in(seeds[6], 71), 0),
        "thermal_noise": bell_draw(seeds[1], (MODES, NY, NX, NZ), 1.0, 4.0, ((1, 16), (2, 8), (3, 4))),
        "relax_rates": jnp.clip(jnp.exp(jax.random.uniform(seeds[2], (MODES,), jnp.float32, math.log(0.4), math.log(1.8))), 0.4, 1.8),
        "plane_shift": set_ends(jax.random.randint(seeds[3], (N_GRAD,), 0, NX), jax.random.fold_in(seeds[3], 1), 0, NX - 1).astype(jnp.int32),
        "fraction_index": jax.random.randint(seeds[4], (1,), 1, FRACS).astype(jnp.int32),
        "plane_speed": jnp.clip(jax.random.uniform(seeds[5], (N_GRAD,), jnp.float32, 0.05, 0.15), 0.05, 0.15),
    }


THERMAL = 0.002

def lattice():
    velocity = np.array([[0, 0, 0], [1, 0, 0], [-1, 0, 0], [0, 1, 0], [0, -1, 0], [0, 0, 1], [0, 0, -1], [1, 1, 0], [-1, -1, 0], [1, -1, 0], [-1, 1, 0], [1, 0, 1], [-1, 0, -1], [1, 0, -1], [-1, 0, 1], [0, 1, 1], [0, -1, -1], [0, 1, -1], [0, -1, 1]]) * 1.0
    weights = np.array([1.0 / 3.0] + [1.0 / 18.0] * 6 + [1.0 / 36.0] * 12)
    axis_x = velocity[:, 0]
    axis_y = velocity[:, 1]
    axis_z = velocity[:, 2]
    monomials = [np.ones(19), axis_x, axis_y, axis_z, axis_x * axis_x, axis_y * axis_y, axis_z * axis_z, axis_x * axis_y, axis_x * axis_z, axis_y * axis_z, axis_x * axis_x * axis_y, axis_x * axis_x * axis_z, axis_y * axis_y * axis_x, axis_y * axis_y * axis_z, axis_z * axis_z * axis_x, axis_z * axis_z * axis_y, axis_x * axis_x * axis_y * axis_y, axis_x * axis_x * axis_z * axis_z, axis_y * axis_y * axis_z * axis_z]
    basis_list = []
    for monomial in monomials:
        vector = monomial.copy()
        for earlier in basis_list:
            vector = vector - np.sum(weights * vector * earlier) / np.sum(weights * earlier * earlier) * earlier
        basis_list.append(vector)
    mode_rows = np.stack(basis_list)
    mode_norms = np.sum(weights[None, :] * mode_rows * mode_rows, axis=1)
    return (velocity, weights, mode_rows, mode_norms)

def collide(flat_pops, flat_noise, relax_rates):
    velocity, weights, mode_rows, mode_norms = lattice()
    highest = lax.Precision.HIGHEST
    moment_table = jnp.asarray(np.concatenate([weights[None, :], weights[None, :] * velocity.T], 0), jnp.float32)
    totals = jnp.dot(moment_table, flat_pops, precision=highest)
    density = totals[0]
    mean_flow = totals[1:] / density[None, :]
    lattice_vel = jnp.asarray(velocity, jnp.float32)
    projected = jnp.dot(lattice_vel, mean_flow, precision=highest)
    speed_sq = lax.optimization_barrier(jnp.sum(mean_flow * mean_flow, axis=0))
    equilibrium = density[None, :] * (1.0 + 3.0 * projected + 4.5 * projected * projected - 1.5 * speed_sq[None, :])
    project_table = jnp.asarray(mode_rows[4:] * weights[None, :], jnp.float32)
    moments = jnp.dot(project_table, flat_pops - equilibrium, precision=highest)
    rate_col = relax_rates[:, None]
    norm_col = jnp.asarray(mode_norms[4:, None], jnp.float32)
    amplitude = jnp.sqrt(THERMAL * density[None, :] * norm_col * rate_col * (2.0 - rate_col))
    relaxed = (1.0 - rate_col) * moments + amplitude * flat_noise.astype(jnp.float32)
    expand_table = jnp.asarray((mode_rows[4:] / mode_norms[4:, None]).T, jnp.float32)
    return (equilibrium + jnp.dot(expand_table, relaxed, precision=highest), density, mean_flow)

def jump_row(direction, dens, flow, amount):
    step_x = float(direction[0])
    step_y = float(direction[1])
    step_z = float(direction[2])
    proj = step_x * flow[0] + step_y * flow[1] + step_z * flow[2]
    return dens * (3.0 * step_x * amount + 9.0 * proj * step_x * amount + 4.5 * step_x * step_x * amount * amount - 3.0 * flow[0] * amount - 1.5 * amount * amount)

def roll_rows(source_plane, amount, extent):
    doubled = jnp.concatenate([source_plane, source_plane], 0)
    begin = ((extent - amount % extent) % extent).astype(jnp.int32)
    return lax.dynamic_slice_in_dim(doubled, begin, extent, 0)

def reference(populations, thermal_noise, relax_rates, plane_shift, fraction_index, plane_speed):
    velocity = lattice()[0]
    pop_blocks = jnp.moveaxis(populations.reshape(19, N_GRAD, -1), 1, 0)
    noise_blocks = jnp.moveaxis(thermal_noise.reshape(15, N_GRAD, -1), 1, 0)
    collided_blocks, dens_blocks, flow_blocks = lax.map(lambda pair: collide(pair[0], pair[1], relax_rates), (pop_blocks, noise_blocks))
    collided = jnp.moveaxis(collided_blocks, 0, 1).reshape(19, NY, NX, NZ)
    dens_slabs = dens_blocks.reshape(N_GRAD, CY, NX, NZ)
    flow_slabs = jnp.moveaxis(flow_blocks, 0, 1).reshape(3, N_GRAD, CY, NX, NZ)
    amount_up = -jnp.roll(plane_speed, -1)[:, None, None]
    amount_down = plane_speed[:, None, None]
    weight_far = fraction_index[0].astype(jnp.float32) / FRACS
    results = []
    for pop_index in range(19):
        step_x = int(velocity[pop_index, 0])
        step_y = int(velocity[pop_index, 1])
        step_z = int(velocity[pop_index, 2])
        plane = collided[pop_index]
        if step_y == 1:
            slabs = plane.reshape(N_GRAD, CY, NX, NZ)
            slabs = slabs.at[:, CY - 1].add(jump_row(velocity[pop_index], dens_slabs[:, CY - 1], flow_slabs[:, :, CY - 1], amount_up))
            plane = slabs.reshape(NY, NX, NZ)
        elif step_y == -1:
            slabs = plane.reshape(N_GRAD, CY, NX, NZ)
            slabs = slabs.at[:, 0].add(jump_row(velocity[pop_index], dens_slabs[:, 0], flow_slabs[:, :, 0], amount_down))
            plane = slabs.reshape(NY, NX, NZ)
        moved = jnp.roll(plane, (step_x, step_z), axis=(1, 2))
        if step_y == 0:
            results.append(moved)
            continue
        moved = jnp.roll(moved, step_y, axis=0)
        slab_rows = moved.reshape(N_GRAD, CY, NX, NZ)
        if step_y == 1:
            source_planes = slab_rows[:, 0]
            plane_shifts = plane_shift.astype(jnp.int32)
            near_part = jax.vmap(lambda one_plane, amount: roll_rows(one_plane, amount, NX))(source_planes, plane_shifts)
            far_part = jax.vmap(lambda one_plane, amount: roll_rows(one_plane, amount + 1, NX))(source_planes, plane_shifts)
            slab_rows = slab_rows.at[:, 0].set((1.0 - weight_far) * near_part + weight_far * far_part)
        else:
            source_planes = slab_rows[:, CY - 1]
            plane_shifts = jnp.roll(plane_shift, -1).astype(jnp.int32)
            near_part = jax.vmap(lambda one_plane, amount: roll_rows(one_plane, -amount, NX))(source_planes, plane_shifts)
            far_part = jax.vmap(lambda one_plane, amount: roll_rows(one_plane, -amount - 1, NX))(source_planes, plane_shifts)
            slab_rows = slab_rows.at[:, CY - 1].set((1.0 - weight_far) * near_part + weight_far * far_part)
        results.append(slab_rows.reshape(NY, NX, NZ))
    return jnp.stack(results)
```

```python
import functools

import jax
import jax.numpy as jnp
import numpy as np
from jax import lax
from jax.experimental import pallas as pl
from jax.experimental.pallas import tpu as pltpu
from jax.sharding import PartitionSpec as P

FRACS = 8
THERMAL = 0.002
MESH = pl.DeviceIdType.MESH

FLOW_UP = (1, 7, 9, 11, 13)
FLOW_DOWN = (2, 8, 10, 12, 14)
FLOW_STAY = (0, 3, 4, 5, 6, 15, 16, 17, 18)
CROSS_UP = (3, 7, 10, 15, 17)
CROSS_DOWN = (4, 8, 9, 18, 16)
VORT_UP = (5, 11, 14, 15, 18)
VORT_DOWN = (6, 12, 13, 16, 17)


def lattice():
    axes = [[1, 0, 0], [0, 1, 0], [0, 0, 1]]
    edges = [[1, 1, 0], [1, -1, 0], [1, 0, 1], [1, 0, -1], [0, 1, 1], [0, 1, -1]]
    rows = [[0, 0, 0]]
    for step in axes + edges:
        rows += [step, [-part for part in step]]
    velocity = np.array(rows) * 1.0
    weights = np.array([1.0 / 3.0] + [1.0 / 18.0] * 6 + [1.0 / 36.0] * 12)
    x, y, z = velocity.T
    monomials = [np.ones(19), x, y, z, x * x, y * y, z * z, x * y, x * z, y * z]
    monomials += [x * x * y, x * x * z, y * y * x, y * y * z, z * z * x, z * z * y]
    monomials += [x * x * y * y, x * x * z * z, y * y * z * z]
    basis = []
    for monomial in monomials:
        vector = monomial.copy()
        for earlier in basis:
            vector = vector - np.sum(weights * vector * earlier) / np.sum(weights * earlier * earlier) * earlier
        basis.append(vector)
    modes = np.stack(basis)
    return velocity, weights, modes, np.sum(weights[None, :] * modes * modes, axis=1)


VELOCITY, WEIGHTS, MODES, NORMS = lattice()
STEPS = VELOCITY.astype(int)
PAIRS = [(i, i + 1) for i in range(1, 19, 2)]
ODD = (1, 2, 3, 10, 11, 12, 13, 14, 15)
EVEN = (0, 4, 5, 6, 7, 8, 9, 16, 17, 18)


def combine(factors, values):
    groups = {}
    for factor, value in zip(factors, values):
        if abs(factor) > 1e-9:
            groups.setdefault(round(abs(float(factor)), 9), []).append((factor, value))
    total = None
    for members in groups.values():
        members.sort(key=lambda member: member[0] < 0)
        lead, part = members[0]
        for factor, value in members[1:]:
            part = part + value if (factor > 0) == (lead > 0) else part - value
        size = abs(float(lead))
        if abs(size - 1.0) > 1e-9:
            part = part * size
        if total is None:
            total = part if lead > 0 else -part
        else:
            total = total + part if lead > 0 else total - part
    return total


def collide(pops, noise, rates, spread):
    sums = [pops[0]] + [pops[a] + pops[b] for a, b in PAIRS]
    gaps = [pops[a] - pops[b] for a, b in PAIRS]
    ids = [0] + [a for a, _ in PAIRS]
    table = MODES * WEIGHTS[None, :]
    moments = {}
    for k in EVEN:
        moments[k] = combine([table[k, i] for i in ids], sums)
    for k in ODD:
        moments[k] = combine([table[k, i] for i in ids[1:]], gaps)
    density = moments[0]
    inverse = 1.0 / density
    flow = [moments[1] * inverse, moments[2] * inverse, moments[3] * inverse]
    root = jnp.sqrt(density)
    second = {}
    for k, (a, b) in zip(range(4, 10), ((0, 0), (1, 1), (2, 2), (0, 1), (0, 2), (1, 2))):
        second[(a, b)] = moments[1 + a] * flow[b]
    scaled = {k: moments[k] * (1.0 / NORMS[k]) for k in range(4)}
    for k in range(4, 19):
        at_rest = None
        if k < 10:
            at_rest = equilibrium_moment(k, second)
        excess = moments[k] if at_rest is None else moments[k] - at_rest
        relaxed = (1.0 - rates[k - 4]) * excess + root * spread(k - 4) * noise(k - 4)
        if at_rest is not None:
            relaxed = relaxed + at_rest
        scaled[k] = relaxed * (1.0 / NORMS[k])
    collided = [None] * 19
    even = [combine([MODES[k, i] for k in EVEN], [scaled[k] for k in EVEN]) for i in ids]
    odd = [combine([MODES[k, i] for k in ODD], [scaled[k] for k in ODD]) for i in ids[1:]]
    collided[0] = even[0]
    for slot, (a, b) in enumerate(PAIRS):
        collided[a] = even[slot + 1] + odd[slot]
        collided[b] = even[slot + 1] - odd[slot]
    return collided, density, flow


def equilibrium_moment(k, second):
    pairs = [(0, 0), (1, 1), (2, 2), (0, 1), (0, 2), (1, 2)]
    factors = []
    for a, b in pairs:
        factor = 4.5 * np.sum(MODES[k] * WEIGHTS * VELOCITY[:, a] * VELOCITY[:, b])
        factors.append(factor if a == b else 2.0 * factor)
    return combine(factors, [second[pair] for pair in pairs])


def jump(pop, density, flow, amount):
    step_x, step_y, step_z = (float(part) for part in STEPS[pop])
    projected = combine((step_x, step_y, step_z), flow)
    inside = -3.0 * amount * flow[0] + (3.0 * step_x * amount - 1.5 * amount * amount)
    if step_x:
        inside = inside + (9.0 * step_x * amount) * projected + 4.5 * amount * amount
    return density * inside


def kernel(
    pop_hbm, noise_hbm, rates_hbm, shift_hbm, frac_hbm, speed_hbm, out,
    pv, nv, rates, shift, frac, speed, spread_ref, upad, dpad, stay,
    send_up, send_down, first_up, first_down, edge_up, edge_down,
    next_up, next_down, window_up, window_down,
    flow_out, flow_in, vort_out, vort_in, square,
    load_sem, send_sem, recv_sem,
):
    g, f, v = lax.axis_index("grad"), lax.axis_index("flow"), lax.axis_index("vort")
    grads, flows, vorts = lax.axis_size("grad"), lax.axis_size("flow"), lax.axis_size("vort")
    half = flows // 2
    side, x = f // half, f % half
    rows = pv.shape[1]

    def place(by_g, by_side, by_x, by_v):
        flow_at = lax.rem(side + by_side, 2) * half + lax.rem(x + by_x + half, half)
        return (lax.rem(g + by_g + grads, grads), flow_at, lax.rem(v + by_v + vorts, vorts))

    def along(by_f):
        return (g, lax.rem(f + by_f + flows, flows), v)

    loads = []

    def load(source, target):
        loads.append(pltpu.make_async_copy(source, target, load_sem.at[len(loads)]))
        loads[-1].start()

    load(pop_hbm.at[:, rows - 1], pv.at[:, rows - 1])
    load(noise_hbm.at[:, rows - 1], nv.at[:, rows - 1])
    load(rates_hbm, rates)
    load(speed_hbm, speed)
    load(pop_hbm.at[:, 0], pv.at[:, 0])
    load(noise_hbm.at[:, 0], nv.at[:, 0])
    load(shift_hbm, shift)
    load(frac_hbm, frac)
    load(pop_hbm.at[:, pl.ds(1, rows - 2)], pv.at[:, pl.ds(1, rows - 2)])
    load(noise_hbm.at[:, pl.ds(1, rows - 2)], nv.at[:, pl.ds(1, rows - 2)])

    partners = [along(1), along(-1), place(0, 0, 0, 1), place(0, 0, 0, -1)]
    partners += [place(0, 0, step, 0) for step in (1, 2, 3)]
    partners += [place(a, b, 0, c) for a in (1, -1) for b in (0, 1) for c in (0, 1, -1)]
    barrier = pltpu.get_barrier_semaphore()
    for partner in partners:
        pl.semaphore_signal(barrier, inc=1, device_id=partner, device_id_type=MESH)

    copies = []

    def send(source, target, device):
        number = len(copies)
        copies.append(
            pltpu.make_async_remote_copy(
                src_ref=source,
                dst_ref=target,
                send_sem=send_sem.at[number],
                recv_sem=recv_sem.at[number],
                device_id=device,
                device_id_type=MESH,
            )
        )
        copies[-1].start()
        return copies[-1]

    lane = lax.broadcasted_iota(jnp.int32, (16, 128), 1)

    def collide_row(y):
        pops = [pv[i, y] for i in range(19)]
        return collide(
            pops,
            lambda k: nv[k, y].astype(jnp.float32),
            [rates[k] for k in range(15)],
            lambda k: jnp.concatenate([spread_ref[k], spread_ref[k]], axis=0),
        )

    def keep(y, collided):
        for slot, pop in enumerate(FLOW_UP):
            upad[slot, y, 8:24, :] = collided[pop]
        for slot, pop in enumerate(FLOW_DOWN):
            dpad[slot, y, 0:16, :] = collided[pop]
        for slot, pop in enumerate(FLOW_STAY):
            stay[slot, y] = collided[pop]

    def first_stage(by_g, rows_out, first, edge):
        return [
            send(rows_out, first.at[1], place(by_g, 1, 0, 0)),
            send(rows_out.at[3], edge.at[1, 0], place(by_g, 1, 0, 1)),
            send(rows_out.at[4], edge.at[1, 1], place(by_g, 1, 0, -1)),
            send(rows_out, first.at[0], place(by_g, 0, 0, 0)),
            send(rows_out.at[3], edge.at[0, 0], place(by_g, 0, 0, 1)),
            send(rows_out.at[4], edge.at[0, 1], place(by_g, 0, 0, -1)),
        ]

    for copy in loads[:4]:
        copy.wait()
    for k in range(15):
        scale = THERMAL * float(NORMS[k + 4]) * rates[k] * (2.0 - rates[k])
        spread_ref[k] = jnp.sqrt(jnp.full((8, 128), scale, jnp.float32))
    collided, density, flow = collide_row(rows - 1)
    amount = -speed[lax.rem(g + 1, grads)]
    for slot, pop in enumerate(CROSS_UP):
        send_up[slot] = collided[pop] + jump(pop, density, flow, amount)
    pl.semaphore_wait(barrier, len(partners))
    up_first = first_stage(1, send_up, first_up, edge_up)
    keep(rows - 1, collided)

    for copy in loads[4:8]:
        copy.wait()
    collided, density, flow = collide_row(0)
    amount = speed[g]
    for slot, pop in enumerate(CROSS_DOWN):
        send_down[slot] = collided[pop] + jump(pop, density, flow, amount)
    down_first = first_stage(-1, send_down, first_down, edge_down)
    keep(0, collided)

    for copy in loads[8:]:
        copy.wait()

    def middle(y, carry):
        keep(y, collide_row(y)[0])
        return carry

    lax.fori_loop(1, rows - 1, middle, 0)

    for slot in range(5):
        for y in range(rows):
            flow_out[0, slot, y : y + 1, :] = upad[slot, y, 23:24, :]
            flow_out[1, slot, y : y + 1, :] = dpad[slot, y, 0:1, :]
    flow_halo = [
        send(flow_out.at[0], flow_in.at[0], along(1)),
        send(flow_out.at[1], flow_in.at[1], along(-1)),
    ]
    for copy in flow_halo:
        copy.wait_recv()
    for slot in range(5):
        for y in range(rows):
            upad[slot, y, 7:8, :] = flow_in[0, slot, y : y + 1, :]
            dpad[slot, y, 16:17, :] = flow_in[1, slot, y : y + 1, :]

    def shifted(pop, y):
        if pop in FLOW_UP:
            return upad[FLOW_UP.index(pop), y, 7:23, :]
        if pop in FLOW_DOWN:
            return dpad[FLOW_DOWN.index(pop), y, 1:17, :]
        return stay[FLOW_STAY.index(pop), y]

    for y in range(rows):
        tile = jnp.zeros((16, 128), jnp.float32)
        for slot, pop in enumerate(VORT_UP):
            tile = jnp.where(lane == slot, pltpu.roll(shifted(pop, y), slot + 1, 1), tile)
        for slot, pop in enumerate(VORT_DOWN):
            tile = jnp.where(lane == 8 + slot, pltpu.roll(shifted(pop, y), 8 + slot, 1), tile)
        square[16 * y : 16 * y + 16, :] = tile
    vort_out[...] = square[...].T[0:16, :]
    vort_halo = [
        send(vort_out.at[pl.ds(0, 8)], vort_in.at[pl.ds(0, 8)], place(0, 0, 0, 1)),
        send(vort_out.at[pl.ds(8, 8)], vort_in.at[pl.ds(8, 8)], place(0, 0, 0, -1)),
    ]

    def target_rows(pop):
        step = int(STEPS[pop, 1])
        return [(y, y + step) for y in range(rows) if 0 <= y + step < rows]

    for pop in range(19):
        if STEPS[pop, 2] == 0:
            for y, to in target_rows(pop):
                out[pop, to] = shifted(pop, y)

    for copy in vort_halo:
        copy.wait_recv()
    square[...] = jnp.concatenate([vort_in[...], jnp.zeros((112, 128), jnp.float32)], axis=0).T
    for slot, (up, down) in enumerate(zip(VORT_UP, VORT_DOWN)):
        for y, to in target_rows(up):
            edge = pltpu.roll(square[16 * y : 16 * y + 16, :], (128 - slot) % 128, 1)
            out[up, to] = jnp.where(lane == 0, edge, pltpu.roll(shifted(up, y), 1, 1))
        for y, to in target_rows(down):
            edge = pltpu.roll(square[16 * y : 16 * y + 16, :], 119 - slot, 1)
            out[down, to] = jnp.where(lane == 127, edge, pltpu.roll(shifted(down, y), 127, 1))

    far = frac[0].astype(jnp.float32) * (1.0 / FRACS)

    def second_stage(arrived, first, edge, onward, window, crossing, offset, sign):
        for copy in arrived:
            copy.wait_recv()
        for which in range(2):
            first[which, 3] = pltpu.roll(jnp.where(lane == 127, edge[which, 0], first[which, 3]), 1, 1)
            first[which, 4] = pltpu.roll(jnp.where(lane == 0, edge[which, 1], first[which, 4]), 127, 1)
        sent = []
        for step in (2, 1, 3, 0):
            to_x = lax.rem(x + sign * step + half, half)
            apart = sign * (to_x - x)
            for slot, pop in enumerate(crossing):
                moved = offset + sign * int(STEPS[pop, 0])
                chosen = ((apart - ((moved & 127) >> 4)) & 7) >> 2
                block = first[chosen, slot]
                if step:
                    onward[step - 1, slot] = block
                else:
                    window[slot, 0:16, :] = block
                    window[slot, 64:80, :] = block
            if step:
                begin = 64 - 16 * step if sign > 0 else 16 * step
                sent.append(
                    send(onward.at[step - 1], window.at[:, pl.ds(begin, 16)], place(0, 0, sign * step, 0))
                )
        return sent

    def finish(arrived, window, crossing, offset, sign, to):
        for copy in arrived:
            copy.wait_recv()
        for slot, pop in enumerate(crossing):
            moved = (offset + sign * int(STEPS[pop, 0])) & 63
            begin = 64 - moved if sign > 0 else moved
            near_part = window[slot, pl.ds(begin, 16), :]
            far_part = window[slot, pl.ds(begin - sign, 16), :]
            out[pop, to] = (1.0 - far) * near_part + far * far_part

    down_offset, up_offset = shift[lax.rem(g + 1, grads)], shift[g]
    down_next = second_stage(down_first, first_down, edge_down, next_down, window_down, CROSS_DOWN, down_offset, -1)
    finish(down_next, window_down, CROSS_DOWN, down_offset, -1, rows - 1)
    up_next = second_stage(up_first, first_up, edge_up, next_up, window_up, CROSS_UP, up_offset, 1)
    finish(up_next, window_up, CROSS_UP, up_offset, 1, 0)
    for copy in copies:
        copy.wait_send()


def on_device(populations, thermal_noise, relax_rates, plane_shift, fraction_index, plane_speed):
    rows = populations.shape[1]
    scratch = [
        pltpu.VMEM(populations.shape, jnp.float32),
        pltpu.VMEM(thermal_noise.shape, jnp.bfloat16),
        pltpu.SMEM(relax_rates.shape, jnp.float32),
        pltpu.SMEM(plane_shift.shape, jnp.int32),
        pltpu.SMEM(fraction_index.shape, jnp.int32),
        pltpu.SMEM(plane_speed.shape, jnp.float32),
        pltpu.VMEM((15, 8, 128), jnp.float32),
        pltpu.VMEM((5, rows, 24, 128), jnp.float32),
        pltpu.VMEM((5, rows, 24, 128), jnp.float32),
        pltpu.VMEM((9, rows, 16, 128), jnp.float32),
        pltpu.VMEM((5, 16, 128), jnp.float32),
        pltpu.VMEM((5, 16, 128), jnp.float32),
        pltpu.VMEM((2, 5, 16, 128), jnp.float32),
        pltpu.VMEM((2, 5, 16, 128), jnp.float32),
        pltpu.VMEM((2, 2, 16, 128), jnp.float32),
        pltpu.VMEM((2, 2, 16, 128), jnp.float32),
        pltpu.VMEM((3, 5, 16, 128), jnp.float32),
        pltpu.VMEM((3, 5, 16, 128), jnp.float32),
        pltpu.VMEM((5, 80, 128), jnp.float32),
        pltpu.VMEM((5, 80, 128), jnp.float32),
        pltpu.VMEM((2, 5, 8, 128), jnp.float32),
        pltpu.VMEM((2, 5, 8, 128), jnp.float32),
        pltpu.VMEM((16, 128), jnp.float32),
        pltpu.VMEM((16, 128), jnp.float32),
        pltpu.VMEM((128, 128), jnp.float32),
        pltpu.SemaphoreType.DMA((10,)),
        pltpu.SemaphoreType.DMA((22,)),
        pltpu.SemaphoreType.DMA((22,)),
    ]
    return pl.pallas_call(
        kernel,
        out_shape=pltpu.VMEM(populations.shape, jnp.float32),
        in_specs=[pl.BlockSpec(memory_space=pltpu.HBM)] * 6,
        out_specs=pl.BlockSpec(memory_space=pltpu.VMEM),
        scratch_shapes=scratch,
        compiler_params=pltpu.CompilerParams(
            collective_id=0, has_side_effects=True, vmem_limit_bytes=24 << 20
        ),
    )(populations, thermal_noise, relax_rates, plane_shift, fraction_index, plane_speed)


def solution(mesh):
    return jax.shard_map(
        on_device,
        mesh=mesh,
        in_specs=(P(None, "grad", "flow", "vort"), P(None, "grad", "flow", "vort"), P(), P(), P(), P()),
        out_specs=P(None, "grad", "flow", "vort"),
        check_vma=False,
    )
```

```python
import functools

import jax
import jax.numpy as jnp
import numpy as np
from jax import lax
from jax.experimental import pallas as pl
from jax.experimental.pallas import tpu as pltpu
from jax.sharding import PartitionSpec as P

FRACS = 8
THERMAL = 0.002
MESH = pl.DeviceIdType.MESH

FLOW_UP = (1, 7, 9, 11, 13)
FLOW_DOWN = (2, 8, 10, 14, 12)
FLOW_STAY = (0, 3, 4, 5, 6, 15, 16, 17, 18)
CROSS_UP = (3, 7, 10, 15, 17)
CROSS_DOWN = (4, 8, 9, 18, 16)
VORT_UP = (5, 11, 14, 15, 18)
VORT_DOWN = (6, 12, 13, 16, 17)


def lattice():
    axes = [[1, 0, 0], [0, 1, 0], [0, 0, 1]]
    edges = [[1, 1, 0], [1, -1, 0], [1, 0, 1], [1, 0, -1], [0, 1, 1], [0, 1, -1]]
    rows = [[0, 0, 0]]
    for step in axes + edges:
        rows += [step, [-part for part in step]]
    velocity = np.array(rows) * 1.0
    weights = np.array([1.0 / 3.0] + [1.0 / 18.0] * 6 + [1.0 / 36.0] * 12)
    x, y, z = velocity.T
    monomials = [np.ones(19), x, y, z, x * x, y * y, z * z, x * y, x * z, y * z]
    monomials += [x * x * y, x * x * z, y * y * x, y * y * z, z * z * x, z * z * y]
    monomials += [x * x * y * y, x * x * z * z, y * y * z * z]
    basis = []
    for monomial in monomials:
        vector = monomial.copy()
        for earlier in basis:
            vector = vector - np.sum(weights * vector * earlier) / np.sum(weights * earlier * earlier) * earlier
        basis.append(vector)
    modes = np.stack(basis)
    return velocity, weights, modes, np.sum(weights[None, :] * modes * modes, axis=1)


VELOCITY, WEIGHTS, MODES, NORMS = lattice()
STEPS = VELOCITY.astype(int)
PAIRS = [(i, i + 1) for i in range(1, 19, 2)]
ODD = (1, 2, 3, 10, 11, 12, 13, 14, 15)
EVEN = (0, 4, 5, 6, 7, 8, 9, 16, 17, 18)


def combine(factors, values):
    groups = {}
    for factor, value in zip(factors, values):
        if abs(factor) > 1e-9:
            groups.setdefault(round(abs(float(factor)), 9), []).append((factor, value))
    total = None
    for members in groups.values():
        members.sort(key=lambda member: member[0] < 0)
        lead, part = members[0]
        for factor, value in members[1:]:
            part = part + value if (factor > 0) == (lead > 0) else part - value
        size = abs(float(lead))
        if abs(size - 1.0) > 1e-9:
            part = part * size
        if total is None:
            total = part if lead > 0 else -part
        else:
            total = total + part if lead > 0 else total - part
    return total


def collide(pops, noise, rates, spread):
    sums = [pops[0]] + [pops[a] + pops[b] for a, b in PAIRS]
    gaps = [pops[a] - pops[b] for a, b in PAIRS]
    ids = [0] + [a for a, _ in PAIRS]
    table = MODES * WEIGHTS[None, :]
    moments = {}
    for k in EVEN:
        moments[k] = combine([table[k, i] for i in ids], sums)
    for k in ODD:
        moments[k] = combine([table[k, i] for i in ids[1:]], gaps)
    density = moments[0]
    inverse = 1.0 / density
    flow = [moments[1] * inverse, moments[2] * inverse, moments[3] * inverse]
    root = jnp.sqrt(density)
    second = {}
    for k, (a, b) in zip(range(4, 10), ((0, 0), (1, 1), (2, 2), (0, 1), (0, 2), (1, 2))):
        second[(a, b)] = moments[1 + a] * flow[b]
    scaled = {k: moments[k] * (1.0 / NORMS[k]) for k in range(4)}
    for k in range(4, 19):
        at_rest = None
        if k < 10:
            at_rest = equilibrium_moment(k, second)
        excess = moments[k] if at_rest is None else moments[k] - at_rest
        relaxed = (1.0 - rates[k - 4]) * excess + root * spread(k - 4) * noise(k - 4)
        if at_rest is not None:
            relaxed = relaxed + at_rest
        scaled[k] = relaxed * (1.0 / NORMS[k])
    collided = [None] * 19
    even = [combine([MODES[k, i] for k in EVEN], [scaled[k] for k in EVEN]) for i in ids]
    odd = [combine([MODES[k, i] for k in ODD], [scaled[k] for k in ODD]) for i in ids[1:]]
    collided[0] = even[0]
    for slot, (a, b) in enumerate(PAIRS):
        collided[a] = even[slot + 1] + odd[slot]
        collided[b] = even[slot + 1] - odd[slot]
    return collided, density, flow


def equilibrium_moment(k, second):
    pairs = [(0, 0), (1, 1), (2, 2), (0, 1), (0, 2), (1, 2)]
    factors = []
    for a, b in pairs:
        factor = 4.5 * np.sum(MODES[k] * WEIGHTS * VELOCITY[:, a] * VELOCITY[:, b])
        factors.append(factor if a == b else 2.0 * factor)
    return combine(factors, [second[pair] for pair in pairs])


def jump(pop, density, flow, amount):
    step_x, step_y, step_z = (float(part) for part in STEPS[pop])
    projected = combine((step_x, step_y, step_z), flow)
    inside = -3.0 * amount * flow[0] + (3.0 * step_x * amount - 1.5 * amount * amount)
    if step_x:
        inside = inside + (9.0 * step_x * amount) * projected + 4.5 * amount * amount
    return density * inside


def kernel(
    pop_hbm, noise_hbm, rates_hbm, shift_hbm, frac, speed_hbm, out,
    pv, nv, rates, shift, speed, spread_ref, upad, dpad, stay,
    send_up, send_down, first_up, first_down, edge_up, edge_down,
    next_up, next_down, window_up, window_down,
    flow_out, flow_in, corner_in, vort_out, vort_in, square,
    load_sem, send_sem, recv_sem, ready_sem,
):
    g, f, v = lax.axis_index("grad"), lax.axis_index("flow"), lax.axis_index("vort")
    grads, flows, vorts = lax.axis_size("grad"), lax.axis_size("flow"), lax.axis_size("vort")
    half = flows // 2
    side, x = f // half, f % half
    rows = pv.shape[1]

    def place(by_g, by_side, by_x, by_v):
        flow_at = lax.rem(side + by_side, 2) * half + lax.rem(x + by_x + half, half)
        return (lax.rem(g + by_g + grads, grads), flow_at, lax.rem(v + by_v + vorts, vorts))

    def along(by_f, by_v):
        return (g, lax.rem(f + by_f + flows, flows), lax.rem(v + by_v + vorts, vorts))

    def across(by_g):
        return [place(by_g, a, 0, c) for a in (1, 0) for c in (0, 1, -1)]

    loads = []

    def load(source, target):
        loads.append(pltpu.make_async_copy(source, target, load_sem.at[len(loads)]))
        loads[-1].start()

    load(pop_hbm.at[:, rows - 1], pv.at[:, rows - 1])
    load(noise_hbm.at[:, rows - 1], nv.at[:, rows - 1])
    load(rates_hbm, rates)
    load(speed_hbm, speed)
    load(pop_hbm.at[:, 0], pv.at[:, 0])
    load(noise_hbm.at[:, 0], nv.at[:, 0])
    load(shift_hbm, shift)
    load(pop_hbm.at[:, pl.ds(1, rows - 2)], pv.at[:, pl.ds(1, rows - 2)])
    load(noise_hbm.at[:, pl.ds(1, rows - 2)], nv.at[:, pl.ds(1, rows - 2)])

    partners = [along(a, c) for a in (-1, 0, 1) for c in (-1, 0, 1) if a or c]
    partners += [place(0, 0, step, 0) for step in (1, 2, 3)]
    barrier = pltpu.get_barrier_semaphore()

    def greet(semaphore, devices):
        for device in devices:
            pl.semaphore_signal(semaphore, inc=1, device_id=device, device_id_type=MESH)

    greet(barrier, partners + across(-1))

    @pl.when(g != grads - 1)
    def _():
        greet(barrier, across(1))

    copies = []

    def send(source, target, device, started=True):
        number = len(copies)
        copies.append(
            pltpu.make_async_remote_copy(
                src_ref=source,
                dst_ref=target,
                send_sem=send_sem.at[number],
                recv_sem=recv_sem.at[number],
                device_id=device,
                device_id_type=MESH,
            )
        )
        if started:
            copies[-1].start()
        return copies[-1]

    lane = lax.broadcasted_iota(jnp.int32, (16, 128), 1)

    def collide_row(y):
        pops = [pv[i, y] for i in range(19)]
        return collide(
            pops,
            lambda k: nv[k, y].astype(jnp.float32),
            [rates[k] for k in range(15)],
            lambda k: jnp.concatenate([spread_ref[k], spread_ref[k]], axis=0),
        )

    def keep(y, collided):
        for slot, pop in enumerate(FLOW_UP):
            upad[slot, y, 8:24, :] = collided[pop]
        for slot, pop in enumerate(FLOW_DOWN):
            dpad[slot, y, 0:16, :] = collided[pop]
        for slot, pop in enumerate(FLOW_STAY):
            stay[slot, y] = collided[pop]

    def first_stage(by_g, rows_out, first, edge, started):
        sent = []
        for which in (1, 0):
            sent.append(send(rows_out, first.at[which], place(by_g, which, 0, 0), started))
            sent.append(send(rows_out.at[3], edge.at[which, 0], place(by_g, which, 0, 1), started))
            sent.append(send(rows_out.at[4], edge.at[which, 1], place(by_g, which, 0, -1), started))
        return sent

    for copy in loads[:4]:
        copy.wait()
    for k in range(15):
        scale = THERMAL * float(NORMS[k + 4]) * rates[k] * (2.0 - rates[k])
        spread_ref[k] = jnp.sqrt(jnp.full((8, 128), scale, jnp.float32))
    collided, density, flow = collide_row(rows - 1)
    amount = -speed[lax.rem(g + 1, grads)]
    for slot, pop in enumerate(CROSS_UP):
        send_up[slot] = collided[pop] + jump(pop, density, flow, amount)

    @pl.when(g == 0)
    def _():
        pl.semaphore_wait(barrier, len(partners) + 6)

    @pl.when(g != 0)
    def _():
        pl.semaphore_wait(barrier, len(partners) + 12)

    up_first = first_stage(1, send_up, first_up, edge_up, True)

    @pl.when(g == grads - 1)
    def _():
        greet(ready_sem, across(1))

    keep(rows - 1, collided)

    for copy in loads[4:7]:
        copy.wait()
    collided, density, flow = collide_row(0)
    amount = speed[g]
    for slot, pop in enumerate(CROSS_DOWN):
        send_down[slot] = collided[pop] + jump(pop, density, flow, amount)
    down_first = first_stage(-1, send_down, first_down, edge_down, False)

    @pl.when(g != 0)
    def _():
        for copy in down_first:
            copy.start()

    keep(0, collided)

    for copy in loads[7:]:
        copy.wait()

    def middle(y, carry):
        keep(y, collide_row(y)[0])
        return carry

    lax.fori_loop(1, rows - 1, middle, 0)

    for slot in range(5):
        for y in range(rows):
            flow_out[0, slot, y : y + 1, :] = upad[slot, y, 23:24, :]
            flow_out[1, slot, y : y + 1, :] = dpad[slot, y, 0:1, :]
    halo = []
    for which, step in enumerate((1, -1)):
        halo.append(send(flow_out.at[which], flow_in.at[which], along(step, 0)))
        halo.append(send(flow_out.at[which, 3], corner_in.at[which, 0], along(step, 1)))
        halo.append(send(flow_out.at[which, 4], corner_in.at[which, 1], along(step, -1)))

    def held(pop):
        if pop in FLOW_UP:
            return upad.at[FLOW_UP.index(pop), :, pl.ds(8, 16), :]
        if pop in FLOW_DOWN:
            return dpad.at[FLOW_DOWN.index(pop), :, pl.ds(0, 16), :]
        return stay.at[FLOW_STAY.index(pop)]

    for y in range(rows):
        tile = jnp.zeros((16, 128), jnp.float32)
        for slot, pop in enumerate(VORT_UP):
            tile = jnp.where(lane == slot, pltpu.roll(held(pop)[y], slot + 1, 1), tile)
        for slot, pop in enumerate(VORT_DOWN):
            tile = jnp.where(lane == 8 + slot, pltpu.roll(held(pop)[y], 8 + slot, 1), tile)
        square[16 * y : 16 * y + 16, :] = tile
    vort_out[...] = square[...].T[0:16, :]
    halo.append(send(vort_out.at[pl.ds(0, 8)], vort_in.at[pl.ds(0, 8)], along(0, 1)))
    halo.append(send(vort_out.at[pl.ds(8, 8)], vort_in.at[pl.ds(8, 8)], along(0, -1)))

    @pl.when(g == 0)
    def _():
        pl.semaphore_wait(ready_sem, 6)
        for copy in down_first:
            copy.start()

    far = frac[0].astype(jnp.float32) * (1.0 / FRACS)

    def second_stage(arrived, first, edge, onward, window, crossing, offset, sign):
        for copy in arrived:
            copy.wait_recv()
        for which in range(2):
            first[which, 3] = pltpu.roll(jnp.where(lane == 127, edge[which, 0], first[which, 3]), 1, 1)
            first[which, 4] = pltpu.roll(jnp.where(lane == 0, edge[which, 1], first[which, 4]), 127, 1)
        sent = []
        for step in (2, 1, 3, 0):
            to_x = lax.rem(x + sign * step + half, half)
            apart = sign * (to_x - x)
            for slot, pop in enumerate(crossing):
                moved = offset + sign * int(STEPS[pop, 0])
                chosen = ((apart - ((moved & 127) >> 4)) & 7) >> 2
                block = first[chosen, slot]
                if step:
                    onward[step - 1, slot] = block
                else:
                    window[slot, 0:16, :] = block
                    window[slot, 64:80, :] = block
            if step:
                begin = 64 - 16 * step if sign > 0 else 16 * step
                sent.append(
                    send(onward.at[step - 1], window.at[:, pl.ds(begin, 16)], place(0, 0, sign * step, 0))
                )
        return sent

    def finish(arrived, window, crossing, offset, sign, to):
        for copy in arrived:
            copy.wait_recv()
        for slot, pop in enumerate(crossing):
            moved = (offset + sign * int(STEPS[pop, 0])) & 63
            begin = 64 - moved if sign > 0 else moved
            near_part = window[slot, pl.ds(begin, 16), :]
            far_part = window[slot, pl.ds(begin - sign, 16), :]
            out[pop, to] = (1.0 - far) * near_part + far * far_part

    down_offset, up_offset = shift[lax.rem(g + 1, grads)], shift[g]
    down_next = second_stage(down_first, first_down, edge_down, next_down, window_down, CROSS_DOWN, down_offset, -1)
    up_next = second_stage(up_first, first_up, edge_up, next_up, window_up, CROSS_UP, up_offset, 1)

    for copy in halo:
        copy.wait_recv()
    square[...] = jnp.concatenate([vort_in[...], jnp.zeros((112, 128), jnp.float32)], axis=0).T

    def target_rows(pop):
        step = int(STEPS[pop, 1])
        return [(y, y + step) for y in range(rows) if 0 <= y + step < rows]

    for pop in range(19):
        for y, to in target_rows(pop):
            here = held(pop)
            value = here[y]
            if pop in VORT_UP:
                edge = pltpu.roll(square[16 * y : 16 * y + 16, :], (128 - VORT_UP.index(pop)) % 128, 1)
                value = jnp.where(lane == 0, edge, pltpu.roll(value, 1, 1))
            elif pop in VORT_DOWN:
                edge = pltpu.roll(square[16 * y : 16 * y + 16, :], 119 - VORT_DOWN.index(pop), 1)
                value = jnp.where(lane == 127, edge, pltpu.roll(value, 127, 1))
            if pop in FLOW_STAY:
                out[pop, to] = value
            elif STEPS[pop, 2]:
                here[y] = value
    for which in range(2):
        joined = jnp.where(lane[0:8] == 127, corner_in[which, 0], flow_in[which, 3])
        flow_in[which, 3] = pltpu.roll(joined, 1, 1)
        joined = jnp.where(lane[0:8] == 0, corner_in[which, 1], flow_in[which, 4])
        flow_in[which, 4] = pltpu.roll(joined, 127, 1)
    for slot, (up, down) in enumerate(zip(FLOW_UP, FLOW_DOWN)):
        for y, to in target_rows(up):
            upad[slot, y, 7:8, :] = flow_in[0, slot, y : y + 1, :]
            out[up, to] = upad[slot, y, 7:23, :]
        for y, to in target_rows(down):
            dpad[slot, y, 16:17, :] = flow_in[1, slot, y : y + 1, :]
            out[down, to] = dpad[slot, y, 1:17, :]
    finish(down_next, window_down, CROSS_DOWN, down_offset, -1, rows - 1)
    finish(up_next, window_up, CROSS_UP, up_offset, 1, 0)
    for copy in copies:
        copy.wait_send()


def pin(whole):
    return pltpu.with_memory_space_constraint(whole, pltpu.HBM)


def on_device(populations, thermal_noise, relax_rates, plane_shift, fraction_index, plane_speed):
    rows = populations.shape[1]
    scratch = [
        pltpu.VMEM(populations.shape, jnp.float32),
        pltpu.VMEM(thermal_noise.shape, jnp.bfloat16),
        pltpu.SMEM(relax_rates.shape, jnp.float32),
        pltpu.SMEM(plane_shift.shape, jnp.int32),
        pltpu.SMEM(plane_speed.shape, jnp.float32),
        pltpu.VMEM((15, 8, 128), jnp.float32),
        pltpu.VMEM((5, rows, 24, 128), jnp.float32),
        pltpu.VMEM((5, rows, 24, 128), jnp.float32),
        pltpu.VMEM((9, rows, 16, 128), jnp.float32),
        pltpu.VMEM((5, 16, 128), jnp.float32),
        pltpu.VMEM((5, 16, 128), jnp.float32),
        pltpu.VMEM((2, 5, 16, 128), jnp.float32),
        pltpu.VMEM((2, 5, 16, 128), jnp.float32),
        pltpu.VMEM((2, 2, 16, 128), jnp.float32),
        pltpu.VMEM((2, 2, 16, 128), jnp.float32),
        pltpu.VMEM((3, 5, 16, 128), jnp.float32),
        pltpu.VMEM((3, 5, 16, 128), jnp.float32),
        pltpu.VMEM((5, 80, 128), jnp.float32),
        pltpu.VMEM((5, 80, 128), jnp.float32),
        pltpu.VMEM((2, 5, 8, 128), jnp.float32),
        pltpu.VMEM((2, 5, 8, 128), jnp.float32),
        pltpu.VMEM((2, 2, 8, 128), jnp.float32),
        pltpu.VMEM((16, 128), jnp.float32),
        pltpu.VMEM((16, 128), jnp.float32),
        pltpu.VMEM((128, 128), jnp.float32),
        pltpu.SemaphoreType.DMA((10,)),
        pltpu.SemaphoreType.DMA((26,)),
        pltpu.SemaphoreType.DMA((26,)),
        pltpu.SemaphoreType.REGULAR,
    ]
    return pl.pallas_call(
        kernel,
        out_shape=pltpu.VMEM(populations.shape, jnp.float32),
        in_specs=[pl.BlockSpec(memory_space=pltpu.SMEM if i == 4 else pltpu.HBM) for i in range(6)],
        out_specs=pl.BlockSpec(memory_space=pltpu.VMEM),
        scratch_shapes=scratch,
        compiler_params=pltpu.CompilerParams(
            collective_id=0, has_side_effects=True, vmem_limit_bytes=24 << 20
        ),
    )(pin(populations), pin(thermal_noise), pin(relax_rates), pin(plane_shift), fraction_index, pin(plane_speed))


def solution(mesh):
    return jax.shard_map(
        on_device,
        mesh=mesh,
        in_specs=(P(None, "grad", "flow", "vort"), P(None, "grad", "flow", "vort"), P(), P(), P(), P()),
        out_specs=P(None, "grad", "flow", "vort"),
        check_vma=False,
    )
```

```python
import functools

import jax
import jax.numpy as jnp
import numpy as np
from jax import lax
from jax.experimental import pallas as pl
from jax.experimental.pallas import tpu as pltpu
from jax.sharding import PartitionSpec as P

FRACS = 8
THERMAL = 0.002
MESH = pl.DeviceIdType.MESH

FLOW_UP = (1, 7, 9, 11, 13)
FLOW_DOWN = (2, 8, 10, 14, 12)
FLOW_STAY = (0, 3, 4, 5, 6, 15, 16, 17, 18)
CROSS_UP = (3, 7, 10, 15, 17)
CROSS_DOWN = (4, 8, 9, 18, 16)
VORT_UP = (5, 11, 14, 15, 18)
VORT_DOWN = (6, 12, 13, 16, 17)


def lattice():
    axes = [[1, 0, 0], [0, 1, 0], [0, 0, 1]]
    edges = [[1, 1, 0], [1, -1, 0], [1, 0, 1], [1, 0, -1], [0, 1, 1], [0, 1, -1]]
    rows = [[0, 0, 0]]
    for step in axes + edges:
        rows += [step, [-part for part in step]]
    velocity = np.array(rows) * 1.0
    weights = np.array([1.0 / 3.0] + [1.0 / 18.0] * 6 + [1.0 / 36.0] * 12)
    x, y, z = velocity.T
    monomials = [np.ones(19), x, y, z, x * x, y * y, z * z, x * y, x * z, y * z]
    monomials += [x * x * y, x * x * z, y * y * x, y * y * z, z * z * x, z * z * y]
    monomials += [x * x * y * y, x * x * z * z, y * y * z * z]
    basis = []
    for monomial in monomials:
        vector = monomial.copy()
        for earlier in basis:
            vector = vector - np.sum(weights * vector * earlier) / np.sum(weights * earlier * earlier) * earlier
        basis.append(vector)
    modes = np.stack(basis)
    return velocity, weights, modes, np.sum(weights[None, :] * modes * modes, axis=1)


VELOCITY, WEIGHTS, MODES, NORMS = lattice()
STEPS = VELOCITY.astype(int)
PAIRS = [(i, i + 1) for i in range(1, 19, 2)]
ODD = (1, 2, 3, 10, 11, 12, 13, 14, 15)
EVEN = (0, 4, 5, 6, 7, 8, 9, 16, 17, 18)


def combine(factors, values):
    groups = {}
    for factor, value in zip(factors, values):
        if abs(factor) > 1e-9:
            groups.setdefault(round(abs(float(factor)), 9), []).append((factor, value))
    total = None
    for members in groups.values():
        members.sort(key=lambda member: member[0] < 0)
        lead, part = members[0]
        for factor, value in members[1:]:
            part = part + value if (factor > 0) == (lead > 0) else part - value
        size = abs(float(lead))
        if abs(size - 1.0) > 1e-9:
            part = part * size
        if total is None:
            total = part if lead > 0 else -part
        else:
            total = total + part if lead > 0 else total - part
    return total


def collide(pops, noise, rates, spread):
    sums = [pops[0]] + [pops[a] + pops[b] for a, b in PAIRS]
    gaps = [pops[a] - pops[b] for a, b in PAIRS]
    ids = [0] + [a for a, _ in PAIRS]
    table = MODES * WEIGHTS[None, :]
    moments = {}
    for k in EVEN:
        moments[k] = combine([table[k, i] for i in ids], sums)
    for k in ODD:
        moments[k] = combine([table[k, i] for i in ids[1:]], gaps)
    density = moments[0]
    inverse = 1.0 / density
    flow = [moments[1] * inverse, moments[2] * inverse, moments[3] * inverse]
    root = jnp.sqrt(density)
    second = {}
    for k, (a, b) in zip(range(4, 10), ((0, 0), (1, 1), (2, 2), (0, 1), (0, 2), (1, 2))):
        second[(a, b)] = moments[1 + a] * flow[b]
    scaled = {k: moments[k] * (1.0 / NORMS[k]) for k in range(4)}
    for k in range(4, 19):
        at_rest = None
        if k < 10:
            at_rest = equilibrium_moment(k, second)
        excess = moments[k] if at_rest is None else moments[k] - at_rest
        relaxed = (1.0 - rates[k - 4]) * excess + root * spread(k - 4) * noise(k - 4)
        if at_rest is not None:
            relaxed = relaxed + at_rest
        scaled[k] = relaxed * (1.0 / NORMS[k])
    collided = [None] * 19
    even = [combine([MODES[k, i] for k in EVEN], [scaled[k] for k in EVEN]) for i in ids]
    odd = [combine([MODES[k, i] for k in ODD], [scaled[k] for k in ODD]) for i in ids[1:]]
    collided[0] = even[0]
    for slot, (a, b) in enumerate(PAIRS):
        collided[a] = even[slot + 1] + odd[slot]
        collided[b] = even[slot + 1] - odd[slot]
    return collided, density, flow


def equilibrium_moment(k, second):
    pairs = [(0, 0), (1, 1), (2, 2), (0, 1), (0, 2), (1, 2)]
    factors = []
    for a, b in pairs:
        factor = 4.5 * np.sum(MODES[k] * WEIGHTS * VELOCITY[:, a] * VELOCITY[:, b])
        factors.append(factor if a == b else 2.0 * factor)
    return combine(factors, [second[pair] for pair in pairs])


def jump(pop, density, flow, amount):
    step_x, step_y, step_z = (float(part) for part in STEPS[pop])
    projected = combine((step_x, step_y, step_z), flow)
    inside = -3.0 * amount * flow[0] + (3.0 * step_x * amount - 1.5 * amount * amount)
    if step_x:
        inside = inside + (9.0 * step_x * amount) * projected + 4.5 * amount * amount
    return density * inside


def kernel(
    pop_hbm, noise_hbm, rates_hbm, shift_hbm, frac, speed_hbm, out,
    pv, nv, rates, shift, speed, spread_ref, upad, dpad, stay,
    send_up, send_down, edge_out_up, edge_out_down, first_up, first_down, late_up, late_down, edge_up, edge_down,
    next_up, next_down, window_up, window_down, window_late_up, window_late_down,
    flow_out, flow_in, corner_in, vort_out, vort_in, square,
    load_sem, send_sem, recv_sem, ready_sem,
):
    g, f, v = lax.axis_index("grad"), lax.axis_index("flow"), lax.axis_index("vort")
    grads, flows, vorts = lax.axis_size("grad"), lax.axis_size("flow"), lax.axis_size("vort")
    half = flows // 2
    side, x = f // half, f % half
    rows = pv.shape[1]

    def place(by_g, by_side, by_x, by_v):
        flow_at = lax.rem(side + by_side, 2) * half + lax.rem(x + by_x + half, half)
        return (lax.rem(g + by_g + grads, grads), flow_at, lax.rem(v + by_v + vorts, vorts))

    def along(by_f, by_v):
        return (g, lax.rem(f + by_f + flows, flows), lax.rem(v + by_v + vorts, vorts))

    def across(by_g):
        return [place(by_g, a, 0, c) for a in (1, 0) for c in (0, 1, -1)]

    loads = []

    def load(source, target):
        loads.append(pltpu.make_async_copy(source, target, load_sem.at[len(loads)]))
        loads[-1].start()

    load(pop_hbm.at[:, rows - 1], pv.at[:, rows - 1])
    load(noise_hbm.at[:, rows - 1], nv.at[:, rows - 1])
    load(rates_hbm, rates)
    load(speed_hbm, speed)
    load(pop_hbm.at[:, 0], pv.at[:, 0])
    load(noise_hbm.at[:, 0], nv.at[:, 0])
    load(shift_hbm, shift)
    load(pop_hbm.at[:, pl.ds(1, rows - 2)], pv.at[:, pl.ds(1, rows - 2)])
    load(noise_hbm.at[:, pl.ds(1, rows - 2)], nv.at[:, pl.ds(1, rows - 2)])

    last = grads - 1
    around = [(a, c) for a in (-1, 0, 1) for c in (-1, 0, 1) if a or c]
    barrier = pltpu.get_barrier_semaphore()

    def greet(semaphore, devices):
        for device in devices:
            pl.semaphore_signal(semaphore, inc=1, device_id=device, device_id_type=MESH)

    def neighbours(slab):
        places = [along(a, c) for a, c in around] + [place(0, 0, step, 0) for step in (1, 2, 3)]
        return [(slab, *rest) for _, *rest in places]

    @pl.when(g == last)
    def _():
        greet(barrier, across(-1) + neighbours(g - 1))

    @pl.when(g != last)
    def _():
        greet(barrier, across(-1) + neighbours(g))

    @pl.when(g < last - 1)
    def _():
        greet(barrier, across(1))

    copies = []

    def send(source, target, device, started=True):
        number = len(copies)
        copies.append(
            pltpu.make_async_remote_copy(
                src_ref=source,
                dst_ref=target,
                send_sem=send_sem.at[number],
                recv_sem=recv_sem.at[number],
                device_id=device,
                device_id_type=MESH,
            )
        )
        if started:
            copies[-1].start()
        return copies[-1]

    lane = lax.broadcasted_iota(jnp.int32, (16, 128), 1)

    def collide_row(y):
        pops = [pv[i, y] for i in range(19)]
        return collide(
            pops,
            lambda k: nv[k, y].astype(jnp.float32),
            [rates[k] for k in range(15)],
            lambda k: jnp.concatenate([spread_ref[k], spread_ref[k]], axis=0),
        )

    def keep(y, collided):
        for slot, pop in enumerate(FLOW_UP):
            upad[slot, y, 8:24, :] = collided[pop]
        for slot, pop in enumerate(FLOW_DOWN):
            dpad[slot, y, 0:16, :] = collided[pop]
        for slot, pop in enumerate(FLOW_STAY):
            stay[slot, y] = collided[pop]

    sub = lax.broadcasted_iota(jnp.int32, (16, 128), 0)

    def turned(column):
        return jnp.sum(jnp.where(lane == sub, column, 0.0), axis=0, keepdims=True)

    def turned_back(row):
        return jnp.sum(jnp.where(lane == sub, row, 0.0), axis=1, keepdims=True)

    def first_stage(by_g, rows_out, edge_out, first, edge, started):
        edge_out[0] = turned(rows_out[3, :, 127:128])
        edge_out[1] = turned(rows_out[4, :, 0:1])
        early, late = [], []
        for which in (1, 0):
            to = place(by_g, which, 0, 0)
            early.append(send(rows_out.at[pl.ds(0, 3)], first[0].at[which], to, started))
        for which in (1, 0):
            late.append(send(edge_out.at[0], edge.at[which, 0], place(by_g, which, 0, 1), started))
            late.append(send(edge_out.at[1], edge.at[which, 1], place(by_g, which, 0, -1), started))
        for which in (1, 0):
            to = place(by_g, which, 0, 0)
            late.append(send(rows_out.at[pl.ds(3, 2)], first[1].at[which], to, started))
        return early, late

    for copy in loads[:4]:
        copy.wait()
    for k in range(15):
        scale = THERMAL * float(NORMS[k + 4]) * rates[k] * (2.0 - rates[k])
        spread_ref[k] = jnp.sqrt(jnp.full((8, 128), scale, jnp.float32))
    collided, density, flow = collide_row(rows - 1)
    amount = -speed[lax.rem(g + 1, grads)]
    for slot, pop in enumerate(CROSS_UP):
        send_up[slot] = collided[pop] + jump(pop, density, flow, amount)

    near = len(around) + 3
    for when, count in ((g == 0, near + 6), ((g > 0) & (g < last - 1), near + 12), (g == last - 1, 2 * near + 12), (g == last, 6)):

        @pl.when(when)
        def _(count=count):
            pl.semaphore_wait(barrier, count)

    up_first = first_stage(1, send_up, edge_out_up, (first_up, late_up), edge_up, True)

    @pl.when(g >= last - 1)
    def _():
        greet(ready_sem, across(1))

    keep(rows - 1, collided)

    for copy in loads[4:7]:
        copy.wait()
    collided, density, flow = collide_row(0)
    amount = speed[g]
    for slot, pop in enumerate(CROSS_DOWN):
        send_down[slot] = collided[pop] + jump(pop, density, flow, amount)
    down_first = first_stage(-1, send_down, edge_out_down, (first_down, late_down), edge_down, False)

    @pl.when((g != 0) & (g != last))
    def _():
        for copy in down_first[0] + down_first[1]:
            copy.start()

    keep(0, collided)

    for copy in loads[7:]:
        copy.wait()

    def middle(y, carry):
        keep(y, collide_row(y)[0])
        return carry

    lax.fori_loop(1, rows - 1, middle, 0)

    for slot in range(5):
        for y in range(rows):
            flow_out[0, slot, y : y + 1, :] = upad[slot, y, 23:24, :]
            flow_out[1, slot, y : y + 1, :] = dpad[slot, y, 0:1, :]

    @pl.when(g == last)
    def _():
        pl.semaphore_wait(ready_sem, 6)
        for copy in down_first[0] + down_first[1]:
            copy.start()

    halo = []
    for which, step in enumerate((1, -1)):
        halo.append(send(flow_out.at[which], flow_in.at[which], along(step, 0)))
        halo.append(send(flow_out.at[which, 3], corner_in.at[which, 0], along(step, 1)))
        halo.append(send(flow_out.at[which, 4], corner_in.at[which, 1], along(step, -1)))

    def held(pop):
        if pop in FLOW_UP:
            return upad.at[FLOW_UP.index(pop), :, pl.ds(8, 16), :]
        if pop in FLOW_DOWN:
            return dpad.at[FLOW_DOWN.index(pop), :, pl.ds(0, 16), :]
        return stay.at[FLOW_STAY.index(pop)]

    for y in range(rows):
        tile = jnp.zeros((16, 128), jnp.float32)
        for slot, pop in enumerate(VORT_UP):
            tile = jnp.where(lane == slot, pltpu.roll(held(pop)[y], slot + 1, 1), tile)
        for slot, pop in enumerate(VORT_DOWN):
            tile = jnp.where(lane == 8 + slot, pltpu.roll(held(pop)[y], 8 + slot, 1), tile)
        square[16 * y : 16 * y + 16, :] = tile
    vort_out[...] = square[...].T[0:16, :]
    halo.append(send(vort_out.at[pl.ds(0, 8)], vort_in.at[pl.ds(0, 8)], along(0, 1)))
    halo.append(send(vort_out.at[pl.ds(8, 8)], vort_in.at[pl.ds(8, 8)], along(0, -1)))

    @pl.when(g == 0)
    def _():
        pl.semaphore_wait(ready_sem, 6)
        for copy in down_first[0] + down_first[1]:
            copy.start()

    far = frac[0].astype(jnp.float32) * (1.0 / FRACS)

    def second_stage(arrived, slots, first, edge, onward, window, crossing, offset, sign):
        for copy in arrived:
            copy.wait_recv()
        if slots[0] == 3:
            for which in range(2):
                upward = pltpu.roll(first[which, 0], 1, 1)
                first[which, 0] = jnp.where(lane == 0, turned_back(edge[which, 0]), upward)
                downward = pltpu.roll(first[which, 1], 127, 1)
                first[which, 1] = jnp.where(lane == 127, turned_back(edge[which, 1]), downward)
        sent = []
        part = pl.ds(slots[0], len(slots))
        for step in (2, 1, 3, 0):
            to_x = lax.rem(x + sign * step + half, half)
            apart = sign * (to_x - x)
            for at, slot in enumerate(slots):
                moved = offset + sign * int(STEPS[crossing[slot], 0])
                chosen = ((apart - ((moved & 127) >> 4)) & 7) >> 2
                block = first[chosen, at]
                if step:
                    onward[step - 1, slot] = block
                else:
                    window[at, 0:16, :] = block
                    window[at, 64:80, :] = block
            if step:
                begin = 64 - 16 * step if sign > 0 else 16 * step
                target = window.at[:, pl.ds(begin, 16)]
                sent.append(send(onward.at[step - 1, part], target, place(0, 0, sign * step, 0)))
        return sent

    def finish(arrived, slots, window, crossing, offset, sign, to):
        for copy in arrived:
            copy.wait_recv()
        for at, slot in enumerate(slots):
            pop = crossing[slot]
            moved = (offset + sign * int(STEPS[pop, 0])) & 63
            begin = 64 - moved if sign > 0 else moved
            near_part = window[at, pl.ds(begin, 16), :]
            far_part = window[at, pl.ds(begin - sign, 16), :]
            out[pop, to] = (1.0 - far) * near_part + far * far_part

    down_offset, up_offset = shift[lax.rem(g + 1, grads)], shift[g]
    nexts = []
    for part, slots in enumerate(((0, 1, 2), (3, 4))):
        down_rest = ((window_down, window_late_down)[part], CROSS_DOWN, down_offset, -1)
        up_rest = ((window_up, window_late_up)[part], CROSS_UP, up_offset, 1)
        down_next = second_stage(down_first[part], slots, (first_down, late_down)[part], edge_down, next_down, *down_rest)
        up_next = second_stage(up_first[part], slots, (first_up, late_up)[part], edge_up, next_up, *up_rest)
        nexts.append((slots, down_next, down_rest, up_next, up_rest))

    for copy in halo:
        copy.wait_recv()
    square[...] = jnp.concatenate([vort_in[...], jnp.zeros((112, 128), jnp.float32)], axis=0).T

    def target_rows(pop):
        step = int(STEPS[pop, 1])
        return [(y, y + step) for y in range(rows) if 0 <= y + step < rows]

    for pop in range(19):
        for y, to in target_rows(pop):
            here = held(pop)
            value = here[y]
            if pop in VORT_UP:
                edge = pltpu.roll(square[16 * y : 16 * y + 16, :], (128 - VORT_UP.index(pop)) % 128, 1)
                value = jnp.where(lane == 0, edge, pltpu.roll(value, 1, 1))
            elif pop in VORT_DOWN:
                edge = pltpu.roll(square[16 * y : 16 * y + 16, :], 119 - VORT_DOWN.index(pop), 1)
                value = jnp.where(lane == 127, edge, pltpu.roll(value, 127, 1))
            if pop in FLOW_STAY:
                out[pop, to] = value
            elif STEPS[pop, 2]:
                here[y] = value
    for which in range(2):
        joined = jnp.where(lane[0:8] == 127, corner_in[which, 0], flow_in[which, 3])
        flow_in[which, 3] = pltpu.roll(joined, 1, 1)
        joined = jnp.where(lane[0:8] == 0, corner_in[which, 1], flow_in[which, 4])
        flow_in[which, 4] = pltpu.roll(joined, 127, 1)
    for slot, (up, down) in enumerate(zip(FLOW_UP, FLOW_DOWN)):
        for y, to in target_rows(up):
            upad[slot, y, 7:8, :] = flow_in[0, slot, y : y + 1, :]
            out[up, to] = upad[slot, y, 7:23, :]
        for y, to in target_rows(down):
            dpad[slot, y, 16:17, :] = flow_in[1, slot, y : y + 1, :]
            out[down, to] = dpad[slot, y, 1:17, :]
    for slots, down_next, down_rest, up_next, up_rest in nexts:
        finish(down_next, slots, *down_rest, rows - 1)
        finish(up_next, slots, *up_rest, 0)
    for copy in copies:
        copy.wait_send()


def pin(whole):
    return pltpu.with_memory_space_constraint(whole, pltpu.HBM)


def on_device(populations, thermal_noise, relax_rates, plane_shift, fraction_index, plane_speed):
    rows = populations.shape[1]
    scratch = [
        pltpu.VMEM(populations.shape, jnp.float32),
        pltpu.VMEM(thermal_noise.shape, jnp.bfloat16),
        pltpu.SMEM(relax_rates.shape, jnp.float32),
        pltpu.SMEM(plane_shift.shape, jnp.int32),
        pltpu.SMEM(plane_speed.shape, jnp.float32),
        pltpu.VMEM((15, 8, 128), jnp.float32),
        pltpu.VMEM((5, rows, 24, 128), jnp.float32),
        pltpu.VMEM((5, rows, 24, 128), jnp.float32),
        pltpu.VMEM((9, rows, 16, 128), jnp.float32),
        pltpu.VMEM((5, 16, 128), jnp.float32),
        pltpu.VMEM((5, 16, 128), jnp.float32),
        pltpu.VMEM((2, 1, 128), jnp.float32),
        pltpu.VMEM((2, 1, 128), jnp.float32),
        pltpu.VMEM((2, 3, 16, 128), jnp.float32),
        pltpu.VMEM((2, 3, 16, 128), jnp.float32),
        pltpu.VMEM((2, 2, 16, 128), jnp.float32),
        pltpu.VMEM((2, 2, 16, 128), jnp.float32),
        pltpu.VMEM((2, 2, 1, 128), jnp.float32),
        pltpu.VMEM((2, 2, 1, 128), jnp.float32),
        pltpu.VMEM((3, 5, 16, 128), jnp.float32),
        pltpu.VMEM((3, 5, 16, 128), jnp.float32),
        pltpu.VMEM((3, 80, 128), jnp.float32),
        pltpu.VMEM((3, 80, 128), jnp.float32),
        pltpu.VMEM((2, 80, 128), jnp.float32),
        pltpu.VMEM((2, 80, 128), jnp.float32),
        pltpu.VMEM((2, 5, 8, 128), jnp.float32),
        pltpu.VMEM((2, 5, 8, 128), jnp.float32),
        pltpu.VMEM((2, 2, 8, 128), jnp.float32),
        pltpu.VMEM((16, 128), jnp.float32),
        pltpu.VMEM((16, 128), jnp.float32),
        pltpu.VMEM((128, 128), jnp.float32),
        pltpu.SemaphoreType.DMA((10,)),
        pltpu.SemaphoreType.DMA((36,)),
        pltpu.SemaphoreType.DMA((36,)),
        pltpu.SemaphoreType.REGULAR,
    ]
    return pl.pallas_call(
        kernel,
        out_shape=pltpu.VMEM(populations.shape, jnp.float32),
        in_specs=[pl.BlockSpec(memory_space=pltpu.SMEM if i == 4 else pltpu.HBM) for i in range(6)],
        out_specs=pl.BlockSpec(memory_space=pltpu.VMEM),
        scratch_shapes=scratch,
        compiler_params=pltpu.CompilerParams(
            collective_id=0, has_side_effects=True, vmem_limit_bytes=24 << 20
        ),
    )(pin(populations), pin(thermal_noise), pin(relax_rates), pin(plane_shift), fraction_index, pin(plane_speed))


def solution(mesh):
    return jax.shard_map(
        on_device,
        mesh=mesh,
        in_specs=(P(None, "grad", "flow", "vort"), P(None, "grad", "flow", "vort"), P(), P(), P(), P()),
        out_specs=P(None, "grad", "flow", "vort"),
        check_vma=False,
    )
```

```python
import math

import jax
import jax.numpy as jnp
import numpy as np
from jax import lax
from jax.experimental import pallas as pl
from jax.experimental.pallas import tpu as pltpu
from jax.sharding import PartitionSpec as P

FRACS = 8
THERMAL = 0.002
MESH = pl.DeviceIdType.MESH

FLOW_UP = (1, 7, 9, 11, 13)
FLOW_DOWN = (2, 8, 10, 14, 12)
FLOW_STAY = (0, 3, 4, 5, 6, 15, 16, 17, 18)
CROSS_UP = (3, 7, 10, 15, 17)
CROSS_DOWN = (4, 8, 9, 18, 16)
VORT_UP = (5, 11, 14, 15, 18)
VORT_DOWN = (6, 12, 13, 16, 17)


def lattice():
    axes = [[1, 0, 0], [0, 1, 0], [0, 0, 1]]
    edges = [[1, 1, 0], [1, -1, 0], [1, 0, 1], [1, 0, -1], [0, 1, 1], [0, 1, -1]]
    rows = [[0, 0, 0]]
    for step in axes + edges:
        rows += [step, [-part for part in step]]
    velocity = np.array(rows) * 1.0
    weights = np.array([1.0 / 3.0] + [1.0 / 18.0] * 6 + [1.0 / 36.0] * 12)
    x, y, z = velocity.T
    monomials = [np.ones(19), x, y, z, x * x, y * y, z * z, x * y, x * z, y * z]
    monomials += [x * x * y, x * x * z, y * y * x, y * y * z, z * z * x, z * z * y]
    monomials += [x * x * y * y, x * x * z * z, y * y * z * z]
    basis = []
    for monomial in monomials:
        vector = monomial.copy()
        for earlier in basis:
            vector = vector - np.sum(weights * vector * earlier) / np.sum(weights * earlier * earlier) * earlier
        basis.append(vector)
    modes = np.stack(basis)
    return velocity, weights, modes, np.sum(weights[None, :] * modes * modes, axis=1)


VELOCITY, WEIGHTS, MODES, NORMS = lattice()
STEPS = VELOCITY.astype(int)
PAIRS = [(i, i + 1) for i in range(1, 19, 2)]
ODD = (1, 2, 3, 10, 11, 12, 13, 14, 15)
EVEN = (0, 4, 5, 6, 7, 8, 9, 16, 17, 18)


def combine(factors, values):
    groups = {}
    for factor, value in zip(factors, values):
        if abs(factor) > 1e-9:
            groups.setdefault(round(abs(float(factor)), 9), []).append((factor, value))
    total = None
    for members in groups.values():
        members.sort(key=lambda member: member[0] < 0)
        lead, part = members[0]
        for factor, value in members[1:]:
            part = part + value if (factor > 0) == (lead > 0) else part - value
        size = abs(float(lead))
        if abs(size - 1.0) > 1e-9:
            part = part * size
        if total is None:
            total = part if lead > 0 else -part
        else:
            total = total + part if lead > 0 else total - part
    return total


def collide(pops, noise, rates, spread):
    sums = [pops[0]] + [pops[a] + pops[b] for a, b in PAIRS]
    gaps = [pops[a] - pops[b] for a, b in PAIRS]
    ids = [0] + [a for a, _ in PAIRS]
    table = MODES * WEIGHTS[None, :]
    moments = {}
    for k in EVEN:
        moments[k] = combine([table[k, i] for i in ids], sums)
    for k in ODD:
        moments[k] = combine([table[k, i] for i in ids[1:]], gaps)
    density = moments[0]
    inverse = 1.0 / density
    flow = [moments[1] * inverse, moments[2] * inverse, moments[3] * inverse]
    root = jnp.sqrt(density)
    second = {}
    for k, (a, b) in zip(range(4, 10), ((0, 0), (1, 1), (2, 2), (0, 1), (0, 2), (1, 2))):
        second[(a, b)] = moments[1 + a] * flow[b]
    scaled = {k: moments[k] * (1.0 / NORMS[k]) for k in range(4)}
    for k in range(4, 19):
        at_rest = None
        if k < 10:
            at_rest = equilibrium_moment(k, second)
        excess = moments[k] if at_rest is None else moments[k] - at_rest
        relaxed = (1.0 - rates[k - 4]) * excess + root * spread(k - 4) * noise(k - 4)
        if at_rest is not None:
            relaxed = relaxed + at_rest
        scaled[k] = relaxed * (1.0 / NORMS[k])
    collided = [None] * 19
    even = [combine([MODES[k, i] for k in EVEN], [scaled[k] for k in EVEN]) for i in ids]
    odd = [combine([MODES[k, i] for k in ODD], [scaled[k] for k in ODD]) for i in ids[1:]]
    collided[0] = even[0]
    for slot, (a, b) in enumerate(PAIRS):
        collided[a] = even[slot + 1] + odd[slot]
        collided[b] = even[slot + 1] - odd[slot]
    return collided, density, flow


def equilibrium_moment(k, second):
    pairs = [(0, 0), (1, 1), (2, 2), (0, 1), (0, 2), (1, 2)]
    factors = []
    for a, b in pairs:
        factor = 4.5 * np.sum(MODES[k] * WEIGHTS * VELOCITY[:, a] * VELOCITY[:, b])
        factors.append(factor if a == b else 2.0 * factor)
    return combine(factors, [second[pair] for pair in pairs])


def jump(pop, density, flow, amount):
    step_x, step_y, step_z = (float(part) for part in STEPS[pop])
    projected = combine((step_x, step_y, step_z), flow)
    inside = -3.0 * amount * flow[0] + (3.0 * step_x * amount - 1.5 * amount * amount)
    if step_x:
        inside = inside + (9.0 * step_x * amount) * projected + 4.5 * amount * amount
    return density * inside


def kernel(
    pop_hbm, noise_hbm, rates_hbm, shift_hbm, frac, speed_hbm, out,
    pv, nv, rates, shift, speed, spread_ref, upad, dpad, stay,
    send_up, send_down, edge_out_up, edge_out_down, first_up, first_down, late_up, late_down, edge_up, edge_down,
    next_up, next_down, window_up, window_down, window_late_up, window_late_down,
    flow_out, flow_in, corner_in, vort_out, vort_in, square, spare,
    load_sem, send_sem, recv_sem, ready_sem,
):
    g, f, v = lax.axis_index("grad"), lax.axis_index("flow"), lax.axis_index("vort")
    grads, flows, vorts = lax.axis_size("grad"), lax.axis_size("flow"), lax.axis_size("vort")
    half = flows // 2
    side, x = f // half, f % half
    rows = pv.shape[1]

    def place(by_g, by_side, by_x, by_v):
        flow_at = lax.rem(side + by_side, 2) * half + lax.rem(x + by_x + half, half)
        return (lax.rem(g + by_g + grads, grads), flow_at, lax.rem(v + by_v + vorts, vorts))

    def along(by_f, by_v):
        return (g, lax.rem(f + by_f + flows, flows), lax.rem(v + by_v + vorts, vorts))

    def across(by_g):
        return [place(by_g, a, 0, c) for a in (1, 0) for c in (0, 1, -1)]

    loads = []

    def load(source, target):
        loads.append(pltpu.make_async_copy(source, target, load_sem.at[len(loads)]))

    load(pop_hbm.at[:, rows - 1], pv.at[:, rows - 1])
    load(noise_hbm.at[:, rows - 1], nv.at[:, rows - 1])
    load(rates_hbm, rates)
    load(speed_hbm, speed)
    load(pop_hbm.at[:, 0], pv.at[:, 0])
    load(noise_hbm.at[:, 0], nv.at[:, 0])
    load(shift_hbm, shift)
    load(pop_hbm.at[:, pl.ds(1, rows - 2)], pv.at[:, pl.ds(1, rows - 2)])
    load(noise_hbm.at[:, pl.ds(1, rows - 2)], nv.at[:, pl.ds(1, rows - 2)])

    last = grads - 1
    around = [(a, c) for a in (-1, 0, 1) for c in (-1, 0, 1) if a or c]
    barrier = pltpu.get_barrier_semaphore()

    def greet(semaphore, devices):
        for device in devices:
            pl.semaphore_signal(semaphore, inc=1, device_id=device, device_id_type=MESH)

    def neighbours(slab):
        places = [along(a, c) for a, c in around] + [place(0, 0, step, 0) for step in (1, 2, 3)]
        return [(slab, *rest) for _, *rest in places]

    for copy in loads[:4]:
        copy.start()

    @pl.when(g != last)
    def _():
        greet(barrier, across(-1) + neighbours(g))
        for copy in loads[4:]:
            copy.start()

    @pl.when(g < last - 1)
    def _():
        greet(barrier, across(1))

    sent_rows, groups = [], {}

    def send(source, target, device, group, started=True):
        sent_rows.append(math.prod(source.shape) // 128)
        groups[group] = groups.get(group, 0) + sent_rows[-1]
        copy = pltpu.make_async_remote_copy(
            src_ref=source,
            dst_ref=target,
            send_sem=send_sem,
            recv_sem=recv_sem.at[list(groups).index(group)],
            device_id=device,
            device_id_type=MESH,
        )
        if started:
            copy.start()
        return copy

    def settle(semaphore, count):
        bytes_of = spare.at[pl.ds(0, count)]
        pltpu.make_async_copy(bytes_of, bytes_of, semaphore).wait()

    def arrive(group):
        settle(recv_sem.at[list(groups).index(group)], groups[group])

    lane = lax.broadcasted_iota(jnp.int32, (16, 128), 1)

    def collide_row(y):
        pops = [pv[i, y] for i in range(19)]
        return collide(
            pops,
            lambda k: nv[k, y].astype(jnp.float32),
            [rates[k] for k in range(15)],
            lambda k: jnp.concatenate([spread_ref[k], spread_ref[k]], axis=0),
        )

    def keep(y, collided):
        for slot, pop in enumerate(FLOW_UP):
            upad[slot, y, 8:24, :] = collided[pop]
        for slot, pop in enumerate(FLOW_DOWN):
            dpad[slot, y, 0:16, :] = collided[pop]
        for slot, pop in enumerate(FLOW_STAY):
            stay[slot, y] = collided[pop]

    sub = lax.broadcasted_iota(jnp.int32, (16, 128), 0)

    def turned(column):
        return jnp.sum(jnp.where(lane == sub, column, 0.0), axis=0, keepdims=True)

    def turned_back(row):
        return jnp.sum(jnp.where(lane == sub, row, 0.0), axis=1, keepdims=True)

    def first_stage(by_g, rows_out, edge_out, first, edge, name, started):
        edge_out[0] = turned(rows_out[3, :, 127:128])
        edge_out[1] = turned(rows_out[4, :, 0:1])
        sent = []
        for which in (1, 0):
            to = place(by_g, which, 0, 0)
            part = name + "0"
            sent.append(send(rows_out.at[pl.ds(3, 2)], first[0].at[which], to, part, started))
            sent.append(send(edge_out.at[0], edge.at[which, 0], place(by_g, which, 0, 1), part, started))
            sent.append(send(edge_out.at[1], edge.at[which, 1], place(by_g, which, 0, -1), part, started))
            sent.append(send(rows_out.at[pl.ds(0, 3)], first[1].at[which], to, name + "1", started))
        return sent

    for copy in loads[:4]:
        copy.wait()
    for k in range(15):
        scale = THERMAL * float(NORMS[k + 4]) * rates[k] * (2.0 - rates[k])
        spread_ref[k] = jnp.sqrt(jnp.full((8, 128), scale, jnp.float32))
    collided, density, flow = collide_row(rows - 1)
    amount = -speed[lax.rem(g + 1, grads)]
    for slot, pop in enumerate(CROSS_UP):
        send_up[slot] = collided[pop] + jump(pop, density, flow, amount)

    near = len(around) + 3
    for when, count in ((g == 0, near + 6), ((g > 0) & (g < last - 1), near + 12), (g == last - 1, 2 * near + 12), (g == last, 6)):

        @pl.when(when)
        def _(count=count):
            pl.semaphore_wait(barrier, count)

    first_stage(1, send_up, edge_out_up, (first_up, late_up), edge_up, "up", True)

    @pl.when(g >= last - 1)
    def _():
        greet(ready_sem, across(1))

    @pl.when(g == last)
    def _():
        greet(barrier, across(-1) + neighbours(g - 1))
        for copy in loads[4:]:
            copy.start()

    keep(rows - 1, collided)

    for copy in loads[4:7]:
        copy.wait()
    collided, density, flow = collide_row(0)
    amount = speed[g]
    for slot, pop in enumerate(CROSS_DOWN):
        send_down[slot] = collided[pop] + jump(pop, density, flow, amount)
    down_first = first_stage(-1, send_down, edge_out_down, (first_down, late_down), edge_down, "down", False)

    @pl.when((g != 0) & (g != last))
    def _():
        for copy in down_first:
            copy.start()

    keep(0, collided)

    for copy in loads[7:]:
        copy.wait()

    def middle(y, carry):
        keep(y, collide_row(y)[0])
        return carry

    lax.fori_loop(1, rows - 1, middle, 0)

    for slot in range(5):
        for y in range(rows):
            flow_out[0, slot, y : y + 1, :] = upad[slot, y, 23:24, :]
            flow_out[1, slot, y : y + 1, :] = dpad[slot, y, 0:1, :]

    @pl.when(g == last)
    def _():
        pl.semaphore_wait(ready_sem, 6)
        for copy in down_first:
            copy.start()

    for which, step in enumerate((1, -1)):
        send(flow_out.at[which], flow_in.at[which], along(step, 0), "halo")
        send(flow_out.at[which, 3], corner_in.at[which, 0], along(step, 1), "halo")
        send(flow_out.at[which, 4], corner_in.at[which, 1], along(step, -1), "halo")

    def held(pop):
        if pop in FLOW_UP:
            return upad.at[FLOW_UP.index(pop), :, pl.ds(8, 16), :]
        if pop in FLOW_DOWN:
            return dpad.at[FLOW_DOWN.index(pop), :, pl.ds(0, 16), :]
        return stay.at[FLOW_STAY.index(pop)]

    for y in range(rows):
        tile = jnp.zeros((16, 128), jnp.float32)
        for slot, pop in enumerate(VORT_UP):
            tile = jnp.where(lane == slot, pltpu.roll(held(pop)[y], slot + 1, 1), tile)
        for slot, pop in enumerate(VORT_DOWN):
            tile = jnp.where(lane == 8 + slot, pltpu.roll(held(pop)[y], 8 + slot, 1), tile)
        square[16 * y : 16 * y + 16, :] = tile
    vort_out[...] = square[...].T[0:16, :]
    send(vort_out.at[pl.ds(0, 8)], vort_in.at[pl.ds(0, 8)], along(0, 1), "halo")
    send(vort_out.at[pl.ds(8, 8)], vort_in.at[pl.ds(8, 8)], along(0, -1), "halo")

    @pl.when(g == 0)
    def _():
        pl.semaphore_wait(ready_sem, 6)
        for copy in down_first:
            copy.start()

    far = frac[0].astype(jnp.float32) * (1.0 / FRACS)

    def second_stage(name, slots, first, edge, onward, window, crossing, offset, sign):
        arrive(name)
        if slots[0] == 3:
            for which in range(2):
                upward = pltpu.roll(first[which, 0], 1, 1)
                first[which, 0] = jnp.where(lane == 0, turned_back(edge[which, 0]), upward)
                downward = pltpu.roll(first[which, 1], 127, 1)
                first[which, 1] = jnp.where(lane == 127, turned_back(edge[which, 1]), downward)
        part = pl.ds(slots[0], len(slots))
        for step in (2, 1, 3, 0):
            to_x = lax.rem(x + sign * step + half, half)
            apart = sign * (to_x - x)
            for at, slot in enumerate(slots):
                moved = offset + sign * int(STEPS[crossing[slot], 0])
                chosen = ((apart - ((moved & 127) >> 4)) & 7) >> 2
                block = first[chosen, at]
                if step:
                    onward[step - 1, slot] = block
                else:
                    window[at, 0:16, :] = block
                    window[at, 64:80, :] = block
            if step:
                begin = 64 - 16 * step if sign > 0 else 16 * step
                target = window.at[:, pl.ds(begin, 16)]
                send(onward.at[step - 1, part], target, place(0, 0, sign * step, 0), name + "next")

    def finish(name, slots, window, crossing, offset, sign, to):
        arrive(name + "next")
        for at, slot in enumerate(slots):
            pop = crossing[slot]
            moved = (offset + sign * int(STEPS[pop, 0])) & 63
            begin = 64 - moved if sign > 0 else moved
            near_part = window[at, pl.ds(begin, 16), :]
            far_part = window[at, pl.ds(begin - sign, 16), :]
            out[pop, to] = (1.0 - far) * near_part + far * far_part

    down_offset, up_offset = shift[lax.rem(g + 1, grads)], shift[g]
    nexts = []
    for part, slots in enumerate(((3, 4), (0, 1, 2))):
        down_rest = ((window_down, window_late_down)[part], CROSS_DOWN, down_offset, -1)
        up_rest = ((window_up, window_late_up)[part], CROSS_UP, up_offset, 1)
        part = str(part)
        second_stage("down" + part, slots, (first_down, late_down)[int(part)], edge_down, next_down, *down_rest)
        second_stage("up" + part, slots, (first_up, late_up)[int(part)], edge_up, next_up, *up_rest)
        nexts.append((part, slots, down_rest, up_rest))

    arrive("halo")
    square[...] = jnp.concatenate([vort_in[...], jnp.zeros((112, 128), jnp.float32)], axis=0).T

    def target_rows(pop):
        step = int(STEPS[pop, 1])
        return [(y, y + step) for y in range(rows) if 0 <= y + step < rows]

    for pop in range(19):
        for y, to in target_rows(pop):
            here = held(pop)
            value = here[y]
            if pop in VORT_UP:
                edge = pltpu.roll(square[16 * y : 16 * y + 16, :], (128 - VORT_UP.index(pop)) % 128, 1)
                value = jnp.where(lane == 0, edge, pltpu.roll(value, 1, 1))
            elif pop in VORT_DOWN:
                edge = pltpu.roll(square[16 * y : 16 * y + 16, :], 119 - VORT_DOWN.index(pop), 1)
                value = jnp.where(lane == 127, edge, pltpu.roll(value, 127, 1))
            if pop in FLOW_STAY:
                out[pop, to] = value
            elif STEPS[pop, 2]:
                here[y] = value
    for which in range(2):
        joined = jnp.where(lane[0:8] == 127, corner_in[which, 0], flow_in[which, 3])
        flow_in[which, 3] = pltpu.roll(joined, 1, 1)
        joined = jnp.where(lane[0:8] == 0, corner_in[which, 1], flow_in[which, 4])
        flow_in[which, 4] = pltpu.roll(joined, 127, 1)
    for slot, (up, down) in enumerate(zip(FLOW_UP, FLOW_DOWN)):
        for y, to in target_rows(up):
            upad[slot, y, 7:8, :] = flow_in[0, slot, y : y + 1, :]
            out[up, to] = upad[slot, y, 7:23, :]
        for y, to in target_rows(down):
            dpad[slot, y, 16:17, :] = flow_in[1, slot, y : y + 1, :]
            out[down, to] = dpad[slot, y, 1:17, :]
    for part, slots, down_rest, up_rest in nexts:
        finish("down" + part, slots, *down_rest, rows - 1)
        finish("up" + part, slots, *up_rest, 0)
    settle(send_sem, sum(sent_rows))


def pin(whole):
    return pltpu.with_memory_space_constraint(whole, pltpu.HBM)


def on_device(populations, thermal_noise, relax_rates, plane_shift, fraction_index, plane_speed):
    rows = populations.shape[1]
    scratch = [
        pltpu.VMEM(populations.shape, jnp.float32),
        pltpu.VMEM(thermal_noise.shape, jnp.bfloat16),
        pltpu.SMEM(relax_rates.shape, jnp.float32),
        pltpu.SMEM(plane_shift.shape, jnp.int32),
        pltpu.SMEM(plane_speed.shape, jnp.float32),
        pltpu.VMEM((15, 8, 128), jnp.float32),
        pltpu.VMEM((5, rows, 24, 128), jnp.float32),
        pltpu.VMEM((5, rows, 24, 128), jnp.float32),
        pltpu.VMEM((9, rows, 16, 128), jnp.float32),
        pltpu.VMEM((5, 16, 128), jnp.float32),
        pltpu.VMEM((5, 16, 128), jnp.float32),
        pltpu.VMEM((2, 1, 128), jnp.float32),
        pltpu.VMEM((2, 1, 128), jnp.float32),
        pltpu.VMEM((2, 2, 16, 128), jnp.float32),
        pltpu.VMEM((2, 2, 16, 128), jnp.float32),
        pltpu.VMEM((2, 3, 16, 128), jnp.float32),
        pltpu.VMEM((2, 3, 16, 128), jnp.float32),
        pltpu.VMEM((2, 2, 1, 128), jnp.float32),
        pltpu.VMEM((2, 2, 1, 128), jnp.float32),
        pltpu.VMEM((3, 5, 16, 128), jnp.float32),
        pltpu.VMEM((3, 5, 16, 128), jnp.float32),
        pltpu.VMEM((2, 80, 128), jnp.float32),
        pltpu.VMEM((2, 80, 128), jnp.float32),
        pltpu.VMEM((3, 80, 128), jnp.float32),
        pltpu.VMEM((3, 80, 128), jnp.float32),
        pltpu.VMEM((2, 5, 8, 128), jnp.float32),
        pltpu.VMEM((2, 5, 8, 128), jnp.float32),
        pltpu.VMEM((2, 2, 8, 128), jnp.float32),
        pltpu.VMEM((16, 128), jnp.float32),
        pltpu.VMEM((16, 128), jnp.float32),
        pltpu.VMEM((128, 128), jnp.float32),
        pltpu.VMEM((1024, 128), jnp.float32),
        pltpu.SemaphoreType.DMA((9,)),
        pltpu.SemaphoreType.DMA,
        pltpu.SemaphoreType.DMA((9,)),
        pltpu.SemaphoreType.REGULAR,
    ]
    return pl.pallas_call(
        kernel,
        out_shape=pltpu.VMEM(populations.shape, jnp.float32),
        in_specs=[pl.BlockSpec(memory_space=pltpu.SMEM if i == 4 else pltpu.HBM) for i in range(6)],
        out_specs=pl.BlockSpec(memory_space=pltpu.VMEM),
        scratch_shapes=scratch,
        compiler_params=pltpu.CompilerParams(
            collective_id=0, has_side_effects=True, vmem_limit_bytes=24 << 20
        ),
    )(pin(populations), pin(thermal_noise), pin(relax_rates), pin(plane_shift), fraction_index, pin(plane_speed))


def solution(mesh):
    return jax.shard_map(
        on_device,
        mesh=mesh,
        in_specs=(P(None, "grad", "flow", "vort"), P(None, "grad", "flow", "vort"), P(), P(), P(), P()),
        out_specs=P(None, "grad", "flow", "vort"),
        check_vma=False,
    )
```

```python
import math

import jax
import jax.numpy as jnp
import numpy as np
from jax import lax
from jax.experimental import pallas as pl
from jax.experimental.pallas import tpu as pltpu
from jax.sharding import PartitionSpec as P

FRACS = 8
THERMAL = 0.002
MESH = pl.DeviceIdType.MESH

FLOW_UP = (1, 7, 9, 11, 13)
FLOW_DOWN = (2, 8, 10, 14, 12)
FLOW_STAY = (0, 3, 4, 5, 6, 15, 16, 17, 18)
CROSS_UP = (3, 7, 10, 15, 17)
CROSS_DOWN = (4, 8, 9, 18, 16)
PARTS = ((0, 1, 2, 3, 4),)
VORT_UP = (5, 11, 14, 15, 18)
VORT_DOWN = (6, 12, 13, 16, 17)


def lattice():
    axes = [[1, 0, 0], [0, 1, 0], [0, 0, 1]]
    edges = [[1, 1, 0], [1, -1, 0], [1, 0, 1], [1, 0, -1], [0, 1, 1], [0, 1, -1]]
    rows = [[0, 0, 0]]
    for step in axes + edges:
        rows += [step, [-part for part in step]]
    velocity = np.array(rows) * 1.0
    weights = np.array([1.0 / 3.0] + [1.0 / 18.0] * 6 + [1.0 / 36.0] * 12)
    x, y, z = velocity.T
    monomials = [np.ones(19), x, y, z, x * x, y * y, z * z, x * y, x * z, y * z]
    monomials += [x * x * y, x * x * z, y * y * x, y * y * z, z * z * x, z * z * y]
    monomials += [x * x * y * y, x * x * z * z, y * y * z * z]
    basis = []
    for monomial in monomials:
        vector = monomial.copy()
        for earlier in basis:
            vector = vector - np.sum(weights * vector * earlier) / np.sum(weights * earlier * earlier) * earlier
        basis.append(vector)
    modes = np.stack(basis)
    return velocity, weights, modes, np.sum(weights[None, :] * modes * modes, axis=1)


VELOCITY, WEIGHTS, MODES, NORMS = lattice()
STEPS = VELOCITY.astype(int)
PAIRS = [(i, i + 1) for i in range(1, 19, 2)]
ODD = (1, 2, 3, 10, 11, 12, 13, 14, 15)
EVEN = (0, 4, 5, 6, 7, 8, 9, 16, 17, 18)


def combine(factors, values):
    groups = {}
    for factor, value in zip(factors, values):
        if abs(factor) > 1e-9:
            groups.setdefault(round(abs(float(factor)), 9), []).append((factor, value))
    total = None
    for members in groups.values():
        members.sort(key=lambda member: member[0] < 0)
        lead, part = members[0]
        for factor, value in members[1:]:
            part = part + value if (factor > 0) == (lead > 0) else part - value
        size = abs(float(lead))
        if abs(size - 1.0) > 1e-9:
            part = part * size
        if total is None:
            total = part if lead > 0 else -part
        else:
            total = total + part if lead > 0 else total - part
    return total


def collide(pops, noise, rates, spread):
    sums = [pops[0]] + [pops[a] + pops[b] for a, b in PAIRS]
    gaps = [pops[a] - pops[b] for a, b in PAIRS]
    ids = [0] + [a for a, _ in PAIRS]
    table = MODES * WEIGHTS[None, :]
    moments = {}
    for k in EVEN:
        moments[k] = combine([table[k, i] for i in ids], sums)
    for k in ODD:
        moments[k] = combine([table[k, i] for i in ids[1:]], gaps)
    density = moments[0]
    inverse = 1.0 / density
    flow = [moments[1] * inverse, moments[2] * inverse, moments[3] * inverse]
    root = jnp.sqrt(density)
    second = {}
    for k, (a, b) in zip(range(4, 10), ((0, 0), (1, 1), (2, 2), (0, 1), (0, 2), (1, 2))):
        second[(a, b)] = moments[1 + a] * flow[b]
    scaled = {k: moments[k] * (1.0 / NORMS[k]) for k in range(4)}
    for k in range(4, 19):
        at_rest = None
        if k < 10:
            at_rest = equilibrium_moment(k, second)
        excess = moments[k] if at_rest is None else moments[k] - at_rest
        relaxed = (1.0 - rates[k - 4]) * excess + root * spread(k - 4) * noise(k - 4)
        if at_rest is not None:
            relaxed = relaxed + at_rest
        scaled[k] = relaxed * (1.0 / NORMS[k])
    collided = [None] * 19
    even = [combine([MODES[k, i] for k in EVEN], [scaled[k] for k in EVEN]) for i in ids]
    odd = [combine([MODES[k, i] for k in ODD], [scaled[k] for k in ODD]) for i in ids[1:]]
    collided[0] = even[0]
    for slot, (a, b) in enumerate(PAIRS):
        collided[a] = even[slot + 1] + odd[slot]
        collided[b] = even[slot + 1] - odd[slot]
    return collided, density, flow


def equilibrium_moment(k, second):
    pairs = [(0, 0), (1, 1), (2, 2), (0, 1), (0, 2), (1, 2)]
    factors = []
    for a, b in pairs:
        factor = 4.5 * np.sum(MODES[k] * WEIGHTS * VELOCITY[:, a] * VELOCITY[:, b])
        factors.append(factor if a == b else 2.0 * factor)
    return combine(factors, [second[pair] for pair in pairs])


def jump(pop, density, flow, amount):
    step_x, step_y, step_z = (float(part) for part in STEPS[pop])
    projected = combine((step_x, step_y, step_z), flow)
    inside = -3.0 * amount * flow[0] + (3.0 * step_x * amount - 1.5 * amount * amount)
    if step_x:
        inside = inside + (9.0 * step_x * amount) * projected + 4.5 * amount * amount
    return density * inside


def kernel(
    pop_hbm, noise_hbm, rates_hbm, shift_hbm, frac, speed_hbm, out,
    pv, nv, rates, shift, speed, spread_ref, upad, dpad, stay,
    send_up, send_down, edge_out_up, edge_out_down, first_up, first_down, edge_up, edge_down,
    next_up, next_down, windows_up, windows_down,
    flow_out, flow_in, corner_in, vort_out, vort_in, square, spare,
    load_sem, send_sem, recv_sem, ready_sem,
):
    g, f, v = lax.axis_index("grad"), lax.axis_index("flow"), lax.axis_index("vort")
    grads, flows, vorts = lax.axis_size("grad"), lax.axis_size("flow"), lax.axis_size("vort")
    half = flows // 2
    side, x = f // half, f % half
    rows = pv.shape[1]

    def place(by_g, by_side, by_x, by_v):
        flow_at = lax.rem(side + by_side, 2) * half + lax.rem(x + by_x + half, half)
        return (lax.rem(g + by_g + grads, grads), flow_at, lax.rem(v + by_v + vorts, vorts))

    def along(by_f, by_v):
        return (g, lax.rem(f + by_f + flows, flows), lax.rem(v + by_v + vorts, vorts))

    def across(by_g):
        return [place(by_g, a, 0, c) for a in (1, 0) for c in (0, 1, -1)]

    loads = []

    def load(source, target):
        loads.append(pltpu.make_async_copy(source, target, load_sem.at[len(loads)]))

    load(pop_hbm.at[:, rows - 1], pv.at[:, rows - 1])
    load(noise_hbm.at[:, rows - 1], nv.at[:, rows - 1])
    load(rates_hbm, rates)
    load(speed_hbm, speed)
    load(pop_hbm.at[:, 0], pv.at[:, 0])
    load(noise_hbm.at[:, 0], nv.at[:, 0])
    load(shift_hbm, shift)
    load(pop_hbm.at[:, pl.ds(1, rows - 2)], pv.at[:, pl.ds(1, rows - 2)])
    load(noise_hbm.at[:, pl.ds(1, rows - 2)], nv.at[:, pl.ds(1, rows - 2)])

    last = grads - 1
    around = [(a, c) for a in (-1, 0, 1) for c in (-1, 0, 1) if a or c]
    barrier = pltpu.get_barrier_semaphore()

    def greet(semaphore, devices):
        for device in devices:
            pl.semaphore_signal(semaphore, inc=1, device_id=device, device_id_type=MESH)

    def neighbours(slab):
        places = [along(a, c) for a, c in around] + [place(0, 0, step, 0) for step in (1, 2, 3)]
        return [(slab, *rest) for _, *rest in places]

    for copy in loads[:4]:
        copy.start()

    @pl.when(g != last)
    def _():
        greet(barrier, across(-1) + neighbours(g))
        for copy in loads[4:]:
            copy.start()

    @pl.when(g < last - 1)
    def _():
        greet(barrier, across(1))

    sent_rows, groups = [], {}

    def send(source, target, device, group, started=True):
        sent_rows.append(math.prod(source.shape) // 128)
        groups[group] = groups.get(group, 0) + sent_rows[-1]
        copy = pltpu.make_async_remote_copy(
            src_ref=source,
            dst_ref=target,
            send_sem=send_sem,
            recv_sem=recv_sem.at[list(groups).index(group)],
            device_id=device,
            device_id_type=MESH,
        )
        if started:
            copy.start()
        return copy

    def settle(semaphore, count):
        bytes_of = spare.at[pl.ds(0, count)]
        pltpu.make_async_copy(bytes_of, bytes_of, semaphore).wait()

    def arrive(group):
        settle(recv_sem.at[list(groups).index(group)], groups[group])

    lane = lax.broadcasted_iota(jnp.int32, (16, 128), 1)

    def collide_row(y):
        pops = [pv[i, y] for i in range(19)]
        return collide(
            pops,
            lambda k: nv[k, y].astype(jnp.float32),
            [rates[k] for k in range(15)],
            lambda k: jnp.concatenate([spread_ref[k], spread_ref[k]], axis=0),
        )

    def keep(y, collided):
        for slot, pop in enumerate(FLOW_UP):
            upad[slot, y, 8:24, :] = collided[pop]
        for slot, pop in enumerate(FLOW_DOWN):
            dpad[slot, y, 0:16, :] = collided[pop]
        for slot, pop in enumerate(FLOW_STAY):
            stay[slot, y] = collided[pop]

    sub = lax.broadcasted_iota(jnp.int32, (16, 128), 0)

    def turned(column):
        return jnp.sum(jnp.where(lane == sub, column, 0.0), axis=0, keepdims=True)

    def turned_back(row):
        return jnp.sum(jnp.where(lane == sub, row, 0.0), axis=1, keepdims=True)

    def first_stage(by_g, rows_out, edge_out, first, edge, name, started):
        edge_out[0] = turned(rows_out[3, :, 127:128])
        edge_out[1] = turned(rows_out[4, :, 0:1])
        sent = []
        for which in (1, 0):
            to = place(by_g, which, 0, 0)
            for part, slots in enumerate(PARTS):
                source = rows_out.at[pl.ds(slots[0], len(slots))]
                sent.append(send(source, first[part].at[which], to, name + str(part), started))
                if part == 0:
                    sent.append(send(edge_out.at[0], edge.at[which, 0], place(by_g, which, 0, 1), name + "0", started))
                    sent.append(send(edge_out.at[1], edge.at[which, 1], place(by_g, which, 0, -1), name + "0", started))
        return sent

    for copy in loads[:4]:
        copy.wait()
    for k in range(15):
        scale = THERMAL * float(NORMS[k + 4]) * rates[k] * (2.0 - rates[k])
        spread_ref[k] = jnp.sqrt(jnp.full((8, 128), scale, jnp.float32))
    collided, density, flow = collide_row(rows - 1)
    amount = -speed[lax.rem(g + 1, grads)]
    for slot, pop in enumerate(CROSS_UP):
        send_up[slot] = collided[pop] + jump(pop, density, flow, amount)

    near = len(around) + 3
    for when, count in ((g == 0, near + 6), ((g > 0) & (g < last - 1), near + 12), (g == last - 1, 2 * near + 12), (g == last, 6)):

        @pl.when(when)
        def _(count=count):
            pl.semaphore_wait(barrier, count)

    first_stage(1, send_up, edge_out_up, first_up, edge_up, "up", True)

    @pl.when(g >= last - 1)
    def _():
        greet(ready_sem, across(1))

    @pl.when(g == last)
    def _():
        greet(barrier, across(-1) + neighbours(g - 1))
        for copy in loads[4:]:
            copy.start()

    keep(rows - 1, collided)

    for copy in loads[4:7]:
        copy.wait()
    collided, density, flow = collide_row(0)
    amount = speed[g]
    for slot, pop in enumerate(CROSS_DOWN):
        send_down[slot] = collided[pop] + jump(pop, density, flow, amount)
    down_first = first_stage(-1, send_down, edge_out_down, first_down, edge_down, "down", False)

    @pl.when((g != 0) & (g != last))
    def _():
        for copy in down_first:
            copy.start()

    keep(0, collided)

    for copy in loads[7:]:
        copy.wait()

    def middle(y, carry):
        keep(y, collide_row(y)[0])
        return carry

    lax.fori_loop(1, rows - 1, middle, 0)

    for slot in range(5):
        for y in range(rows):
            flow_out[0, slot, y : y + 1, :] = upad[slot, y, 23:24, :]
            flow_out[1, slot, y : y + 1, :] = dpad[slot, y, 0:1, :]

    @pl.when(g == last)
    def _():
        pl.semaphore_wait(ready_sem, 6)
        for copy in down_first:
            copy.start()

    for which, step in enumerate((1, -1)):
        send(flow_out.at[which], flow_in.at[which], along(step, 0), "halo")
        send(flow_out.at[which, 3], corner_in.at[which, 0], along(step, 1), "halo")
        send(flow_out.at[which, 4], corner_in.at[which, 1], along(step, -1), "halo")

    def held(pop):
        if pop in FLOW_UP:
            return upad.at[FLOW_UP.index(pop), :, pl.ds(8, 16), :]
        if pop in FLOW_DOWN:
            return dpad.at[FLOW_DOWN.index(pop), :, pl.ds(0, 16), :]
        return stay.at[FLOW_STAY.index(pop)]

    for y in range(rows):
        tile = jnp.zeros((16, 128), jnp.float32)
        for slot, pop in enumerate(VORT_UP):
            tile = jnp.where(lane == slot, pltpu.roll(held(pop)[y], slot + 1, 1), tile)
        for slot, pop in enumerate(VORT_DOWN):
            tile = jnp.where(lane == 8 + slot, pltpu.roll(held(pop)[y], 8 + slot, 1), tile)
        square[16 * y : 16 * y + 16, :] = tile
    vort_out[...] = square[...].T[0:16, :]
    send(vort_out.at[pl.ds(0, 8)], vort_in.at[pl.ds(0, 8)], along(0, 1), "halo")
    send(vort_out.at[pl.ds(8, 8)], vort_in.at[pl.ds(8, 8)], along(0, -1), "halo")

    @pl.when(g == 0)
    def _():
        pl.semaphore_wait(ready_sem, 6)
        for copy in down_first:
            copy.start()

    far = frac[0].astype(jnp.float32) * (1.0 / FRACS)

    def second_stage(name, slots, first, edge, onward, window, crossing, offset, sign):
        arrive(name)
        if 3 in slots:
            at3, at4 = slots.index(3), slots.index(4)
            for which in range(2):
                upward = pltpu.roll(first[which, at3], 1, 1)
                first[which, at3] = jnp.where(lane == 0, turned_back(edge[which, 0]), upward)
                downward = pltpu.roll(first[which, at4], 127, 1)
                first[which, at4] = jnp.where(lane == 127, turned_back(edge[which, 1]), downward)
        part = pl.ds(slots[0], len(slots))
        for step in (2, 1, 3, 0):
            to_x = lax.rem(x + sign * step + half, half)
            apart = sign * (to_x - x)
            for at, slot in enumerate(slots):
                moved = offset + sign * int(STEPS[crossing[slot], 0])
                chosen = ((apart - ((moved & 127) >> 4)) & 7) >> 2
                block = first[chosen, at]
                if step:
                    onward[step - 1, slot] = block
                else:
                    window[at, 0:16, :] = block
                    window[at, 64:80, :] = block
            if step:
                begin = 64 - 16 * step if sign > 0 else 16 * step
                target = window.at[:, pl.ds(begin, 16)]
                send(onward.at[step - 1, part], target, place(0, 0, sign * step, 0), name + "next")

    def finish(name, slots, window, crossing, offset, sign, to):
        arrive(name + "next")
        for at, slot in enumerate(slots):
            pop = crossing[slot]
            moved = (offset + sign * int(STEPS[pop, 0])) & 63
            begin = 64 - moved if sign > 0 else moved
            near_part = window[at, pl.ds(begin, 16), :]
            far_part = window[at, pl.ds(begin - sign, 16), :]
            out[pop, to] = (1.0 - far) * near_part + far * far_part

    down_offset, up_offset = shift[lax.rem(g + 1, grads)], shift[g]
    nexts = []
    for part, slots in enumerate(PARTS):
        down_rest = (windows_down[part], CROSS_DOWN, down_offset, -1)
        up_rest = (windows_up[part], CROSS_UP, up_offset, 1)
        second_stage("down" + str(part), slots, first_down[part], edge_down, next_down, *down_rest)
        second_stage("up" + str(part), slots, first_up[part], edge_up, next_up, *up_rest)
        nexts.append((str(part), slots, down_rest, up_rest))

    arrive("halo")
    square[...] = jnp.concatenate([vort_in[...], jnp.zeros((112, 128), jnp.float32)], axis=0).T

    def target_rows(pop):
        step = int(STEPS[pop, 1])
        return [(y, y + step) for y in range(rows) if 0 <= y + step < rows]

    for pop in range(19):
        for y, to in target_rows(pop):
            here = held(pop)
            value = here[y]
            if pop in VORT_UP:
                edge = pltpu.roll(square[16 * y : 16 * y + 16, :], (128 - VORT_UP.index(pop)) % 128, 1)
                value = jnp.where(lane == 0, edge, pltpu.roll(value, 1, 1))
            elif pop in VORT_DOWN:
                edge = pltpu.roll(square[16 * y : 16 * y + 16, :], 119 - VORT_DOWN.index(pop), 1)
                value = jnp.where(lane == 127, edge, pltpu.roll(value, 127, 1))
            if pop in FLOW_STAY:
                out[pop, to] = value
            elif STEPS[pop, 2]:
                here[y] = value
    for which in range(2):
        joined = jnp.where(lane[0:8] == 127, corner_in[which, 0], flow_in[which, 3])
        flow_in[which, 3] = pltpu.roll(joined, 1, 1)
        joined = jnp.where(lane[0:8] == 0, corner_in[which, 1], flow_in[which, 4])
        flow_in[which, 4] = pltpu.roll(joined, 127, 1)
    for slot, (up, down) in enumerate(zip(FLOW_UP, FLOW_DOWN)):
        for y, to in target_rows(up):
            upad[slot, y, 7:8, :] = flow_in[0, slot, y : y + 1, :]
            out[up, to] = upad[slot, y, 7:23, :]
        for y, to in target_rows(down):
            dpad[slot, y, 16:17, :] = flow_in[1, slot, y : y + 1, :]
            out[down, to] = dpad[slot, y, 1:17, :]
    for part, slots, down_rest, up_rest in nexts:
        finish("down" + part, slots, *down_rest, rows - 1)
        finish("up" + part, slots, *up_rest, 0)
    settle(send_sem, sum(sent_rows))


def pin(whole):
    return pltpu.with_memory_space_constraint(whole, pltpu.HBM)


def on_device(populations, thermal_noise, relax_rates, plane_shift, fraction_index, plane_speed):
    rows = populations.shape[1]
    firsts = [pltpu.VMEM((2, len(slots), 16, 128), jnp.float32) for slots in PARTS]
    windows = [pltpu.VMEM((len(slots), 80, 128), jnp.float32) for slots in PARTS]
    scratch = [
        pltpu.VMEM(populations.shape, jnp.float32),
        pltpu.VMEM(thermal_noise.shape, jnp.bfloat16),
        pltpu.SMEM(relax_rates.shape, jnp.float32),
        pltpu.SMEM(plane_shift.shape, jnp.int32),
        pltpu.SMEM(plane_speed.shape, jnp.float32),
        pltpu.VMEM((15, 8, 128), jnp.float32),
        pltpu.VMEM((5, rows, 24, 128), jnp.float32),
        pltpu.VMEM((5, rows, 24, 128), jnp.float32),
        pltpu.VMEM((9, rows, 16, 128), jnp.float32),
        pltpu.VMEM((5, 16, 128), jnp.float32),
        pltpu.VMEM((5, 16, 128), jnp.float32),
        pltpu.VMEM((2, 1, 128), jnp.float32),
        pltpu.VMEM((2, 1, 128), jnp.float32),
        firsts,
        firsts,
        pltpu.VMEM((2, 2, 1, 128), jnp.float32),
        pltpu.VMEM((2, 2, 1, 128), jnp.float32),
        pltpu.VMEM((3, 5, 16, 128), jnp.float32),
        pltpu.VMEM((3, 5, 16, 128), jnp.float32),
        windows,
        windows,
        pltpu.VMEM((2, 5, 8, 128), jnp.float32),
        pltpu.VMEM((2, 5, 8, 128), jnp.float32),
        pltpu.VMEM((2, 2, 8, 128), jnp.float32),
        pltpu.VMEM((16, 128), jnp.float32),
        pltpu.VMEM((16, 128), jnp.float32),
        pltpu.VMEM((128, 128), jnp.float32),
        pltpu.VMEM((1024, 128), jnp.float32),
        pltpu.SemaphoreType.DMA((9,)),
        pltpu.SemaphoreType.DMA,
        pltpu.SemaphoreType.DMA((9,)),
        pltpu.SemaphoreType.REGULAR,
    ]
    return pl.pallas_call(
        kernel,
        out_shape=pltpu.VMEM(populations.shape, jnp.float32),
        in_specs=[pl.BlockSpec(memory_space=pltpu.SMEM if i == 4 else pltpu.HBM) for i in range(6)],
        out_specs=pl.BlockSpec(memory_space=pltpu.VMEM),
        scratch_shapes=scratch,
        compiler_params=pltpu.CompilerParams(
            collective_id=0, has_side_effects=True, vmem_limit_bytes=24 << 20
        ),
    )(pin(populations), pin(thermal_noise), pin(relax_rates), pin(plane_shift), fraction_index, pin(plane_speed))


def solution(mesh):
    return jax.shard_map(
        on_device,
        mesh=mesh,
        in_specs=(P(None, "grad", "flow", "vort"), P(None, "grad", "flow", "vort"), P(), P(), P(), P()),
        out_specs=P(None, "grad", "flow", "vort"),
        check_vma=False,
    )
```

```python
import math

import jax
import jax.numpy as jnp
import numpy as np
from jax import lax
from jax.experimental import pallas as pl
from jax.experimental.pallas import tpu as pltpu
from jax.sharding import PartitionSpec as P

FRACS = 8
THERMAL = 0.002
MESH = pl.DeviceIdType.MESH

FLOW_UP = (1, 7, 9, 11, 13)
FLOW_DOWN = (2, 8, 10, 14, 12)
FLOW_STAY = (0, 3, 4, 5, 6, 15, 16, 17, 18)
CROSS_UP = (3, 7, 10, 15, 17)
CROSS_DOWN = (4, 8, 9, 18, 16)
PARTS = ((0, 1, 2, 3, 4),)
VORT_UP = (5, 11, 14, 15, 18)
VORT_DOWN = (6, 12, 13, 16, 17)


def lattice():
    axes = [[1, 0, 0], [0, 1, 0], [0, 0, 1]]
    edges = [[1, 1, 0], [1, -1, 0], [1, 0, 1], [1, 0, -1], [0, 1, 1], [0, 1, -1]]
    rows = [[0, 0, 0]]
    for step in axes + edges:
        rows += [step, [-part for part in step]]
    velocity = np.array(rows) * 1.0
    weights = np.array([1.0 / 3.0] + [1.0 / 18.0] * 6 + [1.0 / 36.0] * 12)
    x, y, z = velocity.T
    monomials = [np.ones(19), x, y, z, x * x, y * y, z * z, x * y, x * z, y * z]
    monomials += [x * x * y, x * x * z, y * y * x, y * y * z, z * z * x, z * z * y]
    monomials += [x * x * y * y, x * x * z * z, y * y * z * z]
    basis = []
    for monomial in monomials:
        vector = monomial.copy()
        for earlier in basis:
            vector = vector - np.sum(weights * vector * earlier) / np.sum(weights * earlier * earlier) * earlier
        basis.append(vector)
    modes = np.stack(basis)
    return velocity, weights, modes, np.sum(weights[None, :] * modes * modes, axis=1)


VELOCITY, WEIGHTS, MODES, NORMS = lattice()
STEPS = VELOCITY.astype(int)
PAIRS = [(i, i + 1) for i in range(1, 19, 2)]
ODD = (1, 2, 3, 10, 11, 12, 13, 14, 15)
EVEN = (0, 4, 5, 6, 7, 8, 9, 16, 17, 18)


def combine(factors, values):
    groups = {}
    for factor, value in zip(factors, values):
        if abs(factor) > 1e-9:
            groups.setdefault(round(abs(float(factor)), 9), []).append((factor, value))
    total = None
    for members in groups.values():
        members.sort(key=lambda member: member[0] < 0)
        lead, part = members[0]
        for factor, value in members[1:]:
            part = part + value if (factor > 0) == (lead > 0) else part - value
        size = abs(float(lead))
        if abs(size - 1.0) > 1e-9:
            part = part * size
        if total is None:
            total = part if lead > 0 else -part
        else:
            total = total + part if lead > 0 else total - part
    return total


def collide(pops, noise, rates, spread):
    sums = [pops[0]] + [pops[a] + pops[b] for a, b in PAIRS]
    gaps = [pops[a] - pops[b] for a, b in PAIRS]
    ids = [0] + [a for a, _ in PAIRS]
    table = MODES * WEIGHTS[None, :]
    moments = {}
    for k in EVEN:
        moments[k] = combine([table[k, i] for i in ids], sums)
    for k in ODD:
        moments[k] = combine([table[k, i] for i in ids[1:]], gaps)
    density = moments[0]
    inverse = 1.0 / density
    flow = [moments[1] * inverse, moments[2] * inverse, moments[3] * inverse]
    root = jnp.sqrt(density)
    second = {}
    for k, (a, b) in zip(range(4, 10), ((0, 0), (1, 1), (2, 2), (0, 1), (0, 2), (1, 2))):
        second[(a, b)] = moments[1 + a] * flow[b]
    scaled = {k: moments[k] * (1.0 / NORMS[k]) for k in range(4)}
    for k in range(4, 19):
        at_rest = None
        if k < 10:
            at_rest = equilibrium_moment(k, second)
        excess = moments[k] if at_rest is None else moments[k] - at_rest
        relaxed = (1.0 - rates[k - 4]) * excess + root * spread(k - 4) * noise(k - 4)
        if at_rest is not None:
            relaxed = relaxed + at_rest
        scaled[k] = relaxed * (1.0 / NORMS[k])
    collided = [None] * 19
    even = [combine([MODES[k, i] for k in EVEN], [scaled[k] for k in EVEN]) for i in ids]
    odd = [combine([MODES[k, i] for k in ODD], [scaled[k] for k in ODD]) for i in ids[1:]]
    collided[0] = even[0]
    for slot, (a, b) in enumerate(PAIRS):
        collided[a] = even[slot + 1] + odd[slot]
        collided[b] = even[slot + 1] - odd[slot]
    return collided, density, flow


def equilibrium_moment(k, second):
    pairs = [(0, 0), (1, 1), (2, 2), (0, 1), (0, 2), (1, 2)]
    factors = []
    for a, b in pairs:
        factor = 4.5 * np.sum(MODES[k] * WEIGHTS * VELOCITY[:, a] * VELOCITY[:, b])
        factors.append(factor if a == b else 2.0 * factor)
    return combine(factors, [second[pair] for pair in pairs])


def jump(pop, density, flow, amount):
    step_x, step_y, step_z = (float(part) for part in STEPS[pop])
    projected = combine((step_x, step_y, step_z), flow)
    inside = -3.0 * amount * flow[0] + (3.0 * step_x * amount - 1.5 * amount * amount)
    if step_x:
        inside = inside + (9.0 * step_x * amount) * projected + 4.5 * amount * amount
    return density * inside


def kernel(
    pop_hbm, noise_hbm, rates_hbm, shift_hbm, frac, speed_hbm, out,
    pv, nv, rates, shift, speed, spread_ref, upad, dpad, stay,
    send_up, send_down, edge_out_up, edge_out_down, first_up, first_down, edge_up, edge_down,
    next_up, next_down, windows_up, windows_down,
    flow_out, flow_in, corner_in, vort_out, vort_in, square, spare,
    load_sem, send_sem, recv_sem, ready_sem,
):
    g, f, v = lax.axis_index("grad"), lax.axis_index("flow"), lax.axis_index("vort")
    grads, flows, vorts = lax.axis_size("grad"), lax.axis_size("flow"), lax.axis_size("vort")
    half = flows // 2
    side, x = f // half, f % half
    rows = pv.shape[1]

    def place(by_g, by_side, by_x, by_v):
        flow_at = lax.rem(side + by_side, 2) * half + lax.rem(x + by_x + half, half)
        return (lax.rem(g + by_g + grads, grads), flow_at, lax.rem(v + by_v + vorts, vorts))

    def along(by_f, by_v):
        return (g, lax.rem(f + by_f + flows, flows), lax.rem(v + by_v + vorts, vorts))

    def across(by_g):
        return [place(by_g, a, 0, c) for a in (1, 0) for c in (0, 1, -1)]

    loads = []

    def load(source, target):
        loads.append(pltpu.make_async_copy(source, target, load_sem.at[len(loads)]))

    load(pop_hbm.at[pl.ds(0, 10), rows - 1], pv.at[pl.ds(0, 10), rows - 1])
    load(pop_hbm.at[pl.ds(10, 9), rows - 1], pv.at[pl.ds(10, 9), rows - 1])
    load(noise_hbm.at[:, rows - 1], nv.at[:, rows - 1])
    load(rates_hbm, rates)
    load(speed_hbm, speed)
    load(pop_hbm.at[:, 0], pv.at[:, 0])
    load(noise_hbm.at[:, 0], nv.at[:, 0])
    load(shift_hbm, shift)
    load(pop_hbm.at[:, pl.ds(1, rows - 2)], pv.at[:, pl.ds(1, rows - 2)])
    load(noise_hbm.at[:, pl.ds(1, rows - 2)], nv.at[:, pl.ds(1, rows - 2)])

    last = grads - 1
    around = [(a, c) for a in (-1, 0, 1) for c in (-1, 0, 1) if a or c]
    barrier = pltpu.get_barrier_semaphore()

    def greet(semaphore, devices):
        for device in devices:
            pl.semaphore_signal(semaphore, inc=1, device_id=device, device_id_type=MESH)

    def neighbours(slab):
        places = [along(a, c) for a, c in around] + [place(0, 0, step, 0) for step in (1, 2, 3)]
        return [(slab, *rest) for _, *rest in places]

    for copy in loads[:5]:
        copy.start()

    @pl.when(g != last)
    def _():
        greet(barrier, across(-1) + neighbours(g))
        for copy in loads[5:]:
            copy.start()

    @pl.when(g < last - 1)
    def _():
        greet(barrier, across(1))

    sent_rows, groups = [], {}

    def send(source, target, device, group, started=True):
        sent_rows.append(math.prod(source.shape) // 128)
        groups[group] = groups.get(group, 0) + sent_rows[-1]
        copy = pltpu.make_async_remote_copy(
            src_ref=source,
            dst_ref=target,
            send_sem=send_sem,
            recv_sem=recv_sem.at[list(groups).index(group)],
            device_id=device,
            device_id_type=MESH,
        )
        if started:
            copy.start()
        return copy

    def settle(semaphore, count):
        bytes_of = spare.at[pl.ds(0, count)]
        pltpu.make_async_copy(bytes_of, bytes_of, semaphore).wait()

    def arrive(group):
        settle(recv_sem.at[list(groups).index(group)], groups[group])

    lane = lax.broadcasted_iota(jnp.int32, (16, 128), 1)

    def collide_row(y):
        pops = [pv[i, y] for i in range(19)]
        return collide(
            pops,
            lambda k: nv[k, y].astype(jnp.float32),
            [rates[k] for k in range(15)],
            lambda k: jnp.concatenate([spread_ref[k], spread_ref[k]], axis=0),
        )

    def keep(y, collided):
        for slot, pop in enumerate(FLOW_UP):
            upad[slot, y, 8:24, :] = collided[pop]
        for slot, pop in enumerate(FLOW_DOWN):
            dpad[slot, y, 0:16, :] = collided[pop]
        for slot, pop in enumerate(FLOW_STAY):
            stay[slot, y] = collided[pop]

    sub = lax.broadcasted_iota(jnp.int32, (16, 128), 0)

    def turned(column):
        return jnp.sum(jnp.where(lane == sub, column, 0.0), axis=0, keepdims=True)

    def turned_back(row):
        return jnp.sum(jnp.where(lane == sub, row, 0.0), axis=1, keepdims=True)

    def first_stage(by_g, rows_out, edge_out, first, edge, name, started):
        edge_out[0] = turned(rows_out[3, :, 127:128])
        edge_out[1] = turned(rows_out[4, :, 0:1])
        sent = []
        for which in (1, 0):
            to = place(by_g, which, 0, 0)
            for part, slots in enumerate(PARTS):
                source = rows_out.at[pl.ds(slots[0], len(slots))]
                sent.append(send(source, first[part].at[which], to, name + str(part), started))
                if part == 0:
                    sent.append(send(edge_out.at[0], edge.at[which, 0], place(by_g, which, 0, 1), name + "0", started))
                    sent.append(send(edge_out.at[1], edge.at[which, 1], place(by_g, which, 0, -1), name + "0", started))
        return sent

    for copy in loads[:5]:
        copy.wait()
    for k in range(15):
        scale = THERMAL * float(NORMS[k + 4]) * rates[k] * (2.0 - rates[k])
        spread_ref[k] = jnp.sqrt(jnp.full((8, 128), scale, jnp.float32))
    collided, density, flow = collide_row(rows - 1)
    amount = -speed[lax.rem(g + 1, grads)]
    for slot, pop in enumerate(CROSS_UP):
        send_up[slot] = collided[pop] + jump(pop, density, flow, amount)

    near = len(around) + 3
    for when, count in ((g == 0, near + 6), ((g > 0) & (g < last - 1), near + 12), (g == last - 1, 2 * near + 12), (g == last, 6)):

        @pl.when(when)
        def _(count=count):
            pl.semaphore_wait(barrier, count)

    first_stage(1, send_up, edge_out_up, first_up, edge_up, "up", True)

    @pl.when(g >= last - 1)
    def _():
        greet(ready_sem, across(1))

    @pl.when(g == last)
    def _():
        greet(barrier, across(-1) + neighbours(g - 1))
        for copy in loads[5:]:
            copy.start()

    keep(rows - 1, collided)

    for copy in loads[5:8]:
        copy.wait()
    collided, density, flow = collide_row(0)
    amount = speed[g]
    for slot, pop in enumerate(CROSS_DOWN):
        send_down[slot] = collided[pop] + jump(pop, density, flow, amount)
    down_first = first_stage(-1, send_down, edge_out_down, first_down, edge_down, "down", False)

    @pl.when((g != 0) & (g != last))
    def _():
        for copy in down_first:
            copy.start()

    keep(0, collided)

    for copy in loads[8:]:
        copy.wait()

    def middle(y, carry):
        keep(y, collide_row(y)[0])
        return carry

    lax.fori_loop(1, rows - 1, middle, 0)

    for slot in range(5):
        for y in range(rows):
            flow_out[0, slot, y : y + 1, :] = upad[slot, y, 23:24, :]
            flow_out[1, slot, y : y + 1, :] = dpad[slot, y, 0:1, :]

    @pl.when(g == last)
    def _():
        pl.semaphore_wait(ready_sem, 6)
        for copy in down_first:
            copy.start()

    for which, step in enumerate((1, -1)):
        send(flow_out.at[which], flow_in.at[which], along(step, 0), "halo")
        send(flow_out.at[which, 3], corner_in.at[which, 0], along(step, 1), "halo")
        send(flow_out.at[which, 4], corner_in.at[which, 1], along(step, -1), "halo")

    def held(pop):
        if pop in FLOW_UP:
            return upad.at[FLOW_UP.index(pop), :, pl.ds(8, 16), :]
        if pop in FLOW_DOWN:
            return dpad.at[FLOW_DOWN.index(pop), :, pl.ds(0, 16), :]
        return stay.at[FLOW_STAY.index(pop)]

    for y in range(rows):
        tile = jnp.zeros((16, 128), jnp.float32)
        for slot, pop in enumerate(VORT_UP):
            tile = jnp.where(lane == slot, pltpu.roll(held(pop)[y], slot + 1, 1), tile)
        for slot, pop in enumerate(VORT_DOWN):
            tile = jnp.where(lane == 8 + slot, pltpu.roll(held(pop)[y], 8 + slot, 1), tile)
        square[16 * y : 16 * y + 16, :] = tile
    vort_out[...] = square[...].T[0:16, :]
    send(vort_out.at[pl.ds(0, 8)], vort_in.at[pl.ds(0, 8)], along(0, 1), "halo")
    send(vort_out.at[pl.ds(8, 8)], vort_in.at[pl.ds(8, 8)], along(0, -1), "halo")

    @pl.when(g == 0)
    def _():
        pl.semaphore_wait(ready_sem, 6)
        for copy in down_first:
            copy.start()

    far = frac[0].astype(jnp.float32) * (1.0 / FRACS)

    def second_stage(name, slots, first, edge, onward, window, crossing, offset, sign):
        arrive(name)
        if 3 in slots:
            at3, at4 = slots.index(3), slots.index(4)
            for which in range(2):
                upward = pltpu.roll(first[which, at3], 1, 1)
                first[which, at3] = jnp.where(lane == 0, turned_back(edge[which, 0]), upward)
                downward = pltpu.roll(first[which, at4], 127, 1)
                first[which, at4] = jnp.where(lane == 127, turned_back(edge[which, 1]), downward)
        part = pl.ds(slots[0], len(slots))
        for step in (2, 1, 3, 0):
            to_x = lax.rem(x + sign * step + half, half)
            apart = sign * (to_x - x)
            for at, slot in enumerate(slots):
                moved = offset + sign * int(STEPS[crossing[slot], 0])
                chosen = ((apart - ((moved & 127) >> 4)) & 7) >> 2
                block = first[chosen, at]
                if step:
                    onward[step - 1, slot] = block
                else:
                    window[at, 0:16, :] = block
                    window[at, 64:80, :] = block
            if step:
                begin = 64 - 16 * step if sign > 0 else 16 * step
                target = window.at[:, pl.ds(begin, 16)]
                send(onward.at[step - 1, part], target, place(0, 0, sign * step, 0), name + "next")

    def finish(name, slots, window, crossing, offset, sign, to):
        arrive(name + "next")
        for at, slot in enumerate(slots):
            pop = crossing[slot]
            moved = (offset + sign * int(STEPS[pop, 0])) & 63
            begin = 64 - moved if sign > 0 else moved
            near_part = window[at, pl.ds(begin, 16), :]
            far_part = window[at, pl.ds(begin - sign, 16), :]
            out[pop, to] = (1.0 - far) * near_part + far * far_part

    down_offset, up_offset = shift[lax.rem(g + 1, grads)], shift[g]
    nexts = []
    for part, slots in enumerate(PARTS):
        down_rest = (windows_down[part], CROSS_DOWN, down_offset, -1)
        up_rest = (windows_up[part], CROSS_UP, up_offset, 1)
        second_stage("down" + str(part), slots, first_down[part], edge_down, next_down, *down_rest)
        second_stage("up" + str(part), slots, first_up[part], edge_up, next_up, *up_rest)
        nexts.append((str(part), slots, down_rest, up_rest))

    arrive("halo")
    square[...] = jnp.concatenate([vort_in[...], jnp.zeros((112, 128), jnp.float32)], axis=0).T

    def target_rows(pop):
        step = int(STEPS[pop, 1])
        return [(y, y + step) for y in range(rows) if 0 <= y + step < rows]

    for pop in range(19):
        for y, to in target_rows(pop):
            here = held(pop)
            value = here[y]
            if pop in VORT_UP:
                edge = pltpu.roll(square[16 * y : 16 * y + 16, :], (128 - VORT_UP.index(pop)) % 128, 1)
                value = jnp.where(lane == 0, edge, pltpu.roll(value, 1, 1))
            elif pop in VORT_DOWN:
                edge = pltpu.roll(square[16 * y : 16 * y + 16, :], 119 - VORT_DOWN.index(pop), 1)
                value = jnp.where(lane == 127, edge, pltpu.roll(value, 127, 1))
            if pop in FLOW_STAY:
                out[pop, to] = value
            elif STEPS[pop, 2]:
                here[y] = value
    for which in range(2):
        joined = jnp.where(lane[0:8] == 127, corner_in[which, 0], flow_in[which, 3])
        flow_in[which, 3] = pltpu.roll(joined, 1, 1)
        joined = jnp.where(lane[0:8] == 0, corner_in[which, 1], flow_in[which, 4])
        flow_in[which, 4] = pltpu.roll(joined, 127, 1)
    for slot, (up, down) in enumerate(zip(FLOW_UP, FLOW_DOWN)):
        for y, to in target_rows(up):
            upad[slot, y, 7:8, :] = flow_in[0, slot, y : y + 1, :]
            out[up, to] = upad[slot, y, 7:23, :]
        for y, to in target_rows(down):
            dpad[slot, y, 16:17, :] = flow_in[1, slot, y : y + 1, :]
            out[down, to] = dpad[slot, y, 1:17, :]
    for part, slots, down_rest, up_rest in nexts:
        finish("down" + part, slots, *down_rest, rows - 1)
        finish("up" + part, slots, *up_rest, 0)
    settle(send_sem, sum(sent_rows))


def pin(whole):
    return pltpu.with_memory_space_constraint(whole, pltpu.HBM)


def on_device(populations, thermal_noise, relax_rates, plane_shift, fraction_index, plane_speed):
    rows = populations.shape[1]
    firsts = [pltpu.VMEM((2, len(slots), 16, 128), jnp.float32) for slots in PARTS]
    windows = [pltpu.VMEM((len(slots), 80, 128), jnp.float32) for slots in PARTS]
    scratch = [
        pltpu.VMEM(populations.shape, jnp.float32),
        pltpu.VMEM(thermal_noise.shape, jnp.bfloat16),
        pltpu.SMEM(relax_rates.shape, jnp.float32),
        pltpu.SMEM(plane_shift.shape, jnp.int32),
        pltpu.SMEM(plane_speed.shape, jnp.float32),
        pltpu.VMEM((15, 8, 128), jnp.float32),
        pltpu.VMEM((5, rows, 24, 128), jnp.float32),
        pltpu.VMEM((5, rows, 24, 128), jnp.float32),
        pltpu.VMEM((9, rows, 16, 128), jnp.float32),
        pltpu.VMEM((5, 16, 128), jnp.float32),
        pltpu.VMEM((5, 16, 128), jnp.float32),
        pltpu.VMEM((2, 1, 128), jnp.float32),
        pltpu.VMEM((2, 1, 128), jnp.float32),
        firsts,
        firsts,
        pltpu.VMEM((2, 2, 1, 128), jnp.float32),
        pltpu.VMEM((2, 2, 1, 128), jnp.float32),
        pltpu.VMEM((3, 5, 16, 128), jnp.float32),
        pltpu.VMEM((3, 5, 16, 128), jnp.float32),
        windows,
        windows,
        pltpu.VMEM((2, 5, 8, 128), jnp.float32),
        pltpu.VMEM((2, 5, 8, 128), jnp.float32),
        pltpu.VMEM((2, 2, 8, 128), jnp.float32),
        pltpu.VMEM((16, 128), jnp.float32),
        pltpu.VMEM((16, 128), jnp.float32),
        pltpu.VMEM((128, 128), jnp.float32),
        pltpu.VMEM((1024, 128), jnp.float32),
        pltpu.SemaphoreType.DMA((10,)),
        pltpu.SemaphoreType.DMA,
        pltpu.SemaphoreType.DMA((9,)),
        pltpu.SemaphoreType.REGULAR,
    ]
    return pl.pallas_call(
        kernel,
        out_shape=pltpu.VMEM(populations.shape, jnp.float32),
        in_specs=[pl.BlockSpec(memory_space=pltpu.SMEM if i == 4 else pltpu.HBM) for i in range(6)],
        out_specs=pl.BlockSpec(memory_space=pltpu.VMEM),
        scratch_shapes=scratch,
        compiler_params=pltpu.CompilerParams(
            collective_id=0, has_side_effects=True, vmem_limit_bytes=24 << 20
        ),
    )(pin(populations), pin(thermal_noise), pin(relax_rates), pin(plane_shift), fraction_index, pin(plane_speed))


def solution(mesh):
    return jax.shard_map(
        on_device,
        mesh=mesh,
        in_specs=(P(None, "grad", "flow", "vort"), P(None, "grad", "flow", "vort"), P(), P(), P(), P()),
        out_specs=P(None, "grad", "flow", "vort"),
        check_vma=False,
    )
```
